128 devices in a mesh: section: 4 (over x), dp: 32 (over z, y, core).
Axes of the slice: x: 4, y: 4, z: 4, core: 2. Of those that a mesh axis runs over, the one named last changes fastest.
Arguments:
- inputs: bfloat16 [4, 5120, 1024], P(None, 'dp'), may hold values from -6 to 6
- cotangent: bfloat16 [4, 5120, 1024], P(None, 'dp'), may hold values from -6 to 6
- layout: int32 [4, 32, 3], P(None, 'dp'), may hold values from 0 to 2, as said below
- pos_index: int32 [144, 4], replicated, may hold values from 1 to 49
- pos_table: bfloat16 [50, 1024], replicated, may hold values from -3 to 3
- slab_in: bfloat16 [4, 1024, 4096], P('section'), as said below
- slab_out: bfloat16 [4, 4096, 1024], P('section'), may hold values from -0.09375 to 0.09375
- bias_in: bfloat16 [4, 4096], P('section'), may hold values from -2 to 2
- bias_out: bfloat16 [4, 1024], P('section'), may hold values from -2 to 2
- ln_gain: bfloat16 [4, 1024], P('section'), may hold values from 0.099609375 to 1.8984375
- ln_bias: bfloat16 [4, 1024], P('section'), may hold values from -2 to 2
Outputs:
- layer_out: bfloat16 [4, 5120, 1024], P(None, 'dp', 'section')
- input_grad: bfloat16 [4, 5120, 1024], P(None, 'dp', 'section')
- grad_slab_in: float32 [4, 1024, 4096], P('section', 'dp')
- grad_slab_out: float32 [4, 4096, 1024], P('section', 'dp')
- grad_bias_in: float32 [4, 4096], P('section', 'dp')
- grad_bias_out: float32 [4, 1024], P('section', 'dp')
- grad_ln_gain: float32 [4, 1024], P('section', 'dp')
- grad_ln_bias: float32 [4, 1024], P('section', 'dp')
- grad_pos: float32 [50, 1024], P(None, ('section', 'dp'))
- stats: float32 [2, 4], replicated
The draws below stay inside these ranges and needn't reach their ends.
Inputs may be any that keep to these rules, and one draw needn't show every extreme that they name: `layout`: slot kinds: 1 an image of 50 tokens, 2 one of 145, 0 no image. The lengths of a buffer's images sum to at most 160, and slot 0 always holds an image. `slab_in`: entries of mean 0 and about unit spread times a constant factor per column block.
All inputs are finite; a program needn't handle non-finite values.
Results may differ from the reference program's by a relative error of at most 0.025.
Values may be sent and summed in bfloat16 or wider, within the bound.
A program may use at most 256 MiB of HBM per device.

```python
import jax
import jax.numpy as jnp
from jax import lax

D = 1024
HEADS = 16
HEAD_DIM = 64
FF = 4096
SHORT = 50
LONG = 145
CORNERS = 4
LAYERS = 2
MICRO = 4
ROWS = 160
SLOTS = 3
BATCH_ROWS = 5120


def draw_slab_in(key, part):
    key = jax.random.fold_in(key, 11)
    base_values = jnp.clip(jax.random.normal(key, (2 * LAYERS, D, FF), jnp.float32), -6.0, 6.0)
    sublayer_ids = jnp.arange(2 * LAYERS)[:, None, None]
    column_ids = jnp.arange(FF)[None, None, :]
    boost = jnp.where((sublayer_ids % 2 == 0) & (column_ids >= 2 * D) & (column_ids < 3 * D), 6.0, 1.0)
    return (base_values * boost * D ** (-0.5)).astype(jnp.bfloat16)


def draw_layout(key, part):
    key = jax.random.fold_in(key, 5)
    buffer_count = BATCH_ROWS // ROWS
    image_kinds = jax.random.randint(key, (MICRO, buffer_count, SLOTS), 1, 3).astype(jnp.int32)
    lengths = jnp.where(image_kinds == 1, SHORT, LONG).astype(jnp.int32)
    used_rows = jnp.zeros((MICRO, buffer_count), jnp.int32)
    columns = []
    for slot_id in range(SLOTS):
        fits = used_rows + lengths[:, :, slot_id] <= ROWS
        columns.append(jnp.where(fits, image_kinds[:, :, slot_id], 0).astype(jnp.int32))
        used_rows = used_rows + jnp.where(fits, lengths[:, :, slot_id], 0).astype(jnp.int32)
    return jnp.stack(columns, axis=2).astype(jnp.int32)


def set_ends(values, stream_key, smallest, top_value):
    place = [jax.random.randint(jax.random.fold_in(stream_key, axis), (), 0, length) for axis, length in enumerate(values.shape)]
    widest = values.shape.index(max(values.shape))
    neighbour = place[:widest] + [(place[widest] + 1) % values.shape[widest]] + place[widest + 1:]
    return values.at[tuple(place)].set(smallest).at[tuple(neighbour)].set(top_value)


def block_levels(key, dims, cuts, least, high):
    loudness, own = 1.0, jax.random.fold_in(key, 6)
    for position, blocks in cuts:
        draws = jnp.exp(jax.random.uniform(jax.random.fold_in(own, position), (blocks,), jnp.float32, least / len(cuts), high / len(cuts)))
        loudness = loudness * jnp.repeat(draws, dims[position] // blocks).reshape([-1 if axis == position else 1 for axis in range(len(dims))])
    return loudness


def gaussian(key, shape, scale, most, cuts=(), kind=jnp.bfloat16):
    values = scale * jax.random.normal(key, shape, jnp.float32)
    if cuts:
        values = values * block_levels(key, shape, cuts, -0.22, 0.18)
    return jnp.clip(values, -most, most).astype(kind)


def setup_inputs(seed: int = 0) -> dict:
    keys = jax.random.split(jax.random.key(seed), 12)
    return {
        "inputs": gaussian(keys[0], (MICRO, BATCH_ROWS, D), 1.0, 6.0, ((1, 32),)),
        "cotangent": gaussian(keys[1], (MICRO, BATCH_ROWS, D), 1.0, 6.0, ((1, 32),)),
        "layout": draw_layout(jax.random.fold_in(keys[11], 71), 0),
        "pos_index": set_ends(jax.random.randint(keys[3], (LONG - 1, CORNERS), 1, SHORT), jax.random.fold_in(keys[3], 1), 1, SHORT - 1).astype(jnp.int32),
        "pos_table": gaussian(keys[4], (SHORT, D), 0.5, 3.0),
        "slab_in": draw_slab_in(jax.random.fold_in(keys[11], 71), 0),
        "slab_out": gaussian(keys[6], (2 * LAYERS, FF, D), FF ** -0.5, 0.09375, ((0, 4),)),
        "bias_in": gaussian(keys[7], (2 * LAYERS, FF), 0.3, 2.0, ((0, 4),)),
        "bias_out": gaussian(keys[8], (2 * LAYERS, D), 0.3, 2.0, ((0, 4),)),
        "ln_gain": jnp.clip(1.0 + 0.18 * jax.random.normal(keys[9], (2 * LAYERS, D), jnp.float32), 0.099609375, 1.8984375).astype(jnp.bfloat16),
        "ln_bias": gaussian(keys[10], (2 * LAYERS, D), 0.3, 2.0, ((0, 4),)),
    }


@jax.custom_vjp
def low(v):
    return lax.optimization_barrier(v.astype(jnp.bfloat16)).astype(jnp.float32)

@jax.custom_vjp
def low_back(v):
    return v

def low_keep(v):
    return (low(v), None)

def low_pass(kept, grad):
    return (grad,)

def back_keep(v):
    return (v, None)

def back_low(kept, grad):
    return (low(grad),)
low.defvjp(low_keep, low_pass)
low_back.defvjp(back_keep, back_low)
LN_EPSILON = 1e-06
FULL_PRECISION = lax.Precision.HIGHEST
MASKED_SCORE = -1e+30

def corner_weights(corner_count):
    order_ids = jnp.arange(corner_count, dtype=jnp.float32)
    return (corner_count - order_ids) / (corner_count * (corner_count + 1) / 2.0)

def tables(layout_row, pos_index, row_count):
    row_ids = jnp.arange(row_count, dtype=jnp.int32)
    lengths = jnp.where(layout_row == 1, SHORT, jnp.where(layout_row == 2, LONG, 0)).astype(jnp.int32)
    starts = (jnp.cumsum(lengths) - lengths).astype(jnp.int32)
    inside = ((row_ids[None, :] >= starts[:, None]) & (row_ids[None, :] < (starts + lengths)[:, None])).astype(jnp.int32)
    slot_ids = jnp.arange(layout_row.shape[0], dtype=jnp.int32)
    segment = (lax.optimization_barrier(jnp.sum(inside * (slot_ids[:, None] + 1), axis=0)) - 1).astype(jnp.int32)
    offset = lax.optimization_barrier(jnp.sum(inside * (row_ids[None, :] - starts[:, None]), axis=0)).astype(jnp.int32)
    long_rows = lax.optimization_barrier(jnp.sum(inside * (layout_row[:, None] == 2).astype(jnp.int32), axis=0)).astype(jnp.int32)
    valid = segment >= 0
    table_ids = jnp.arange(SHORT, dtype=jnp.int32)
    direct = (offset[:, None] == table_ids[None, :]).astype(jnp.float32)
    corner_ids = jnp.take(pos_index, jnp.clip(offset - 1, 0, pos_index.shape[0] - 1), axis=0).astype(jnp.int32)
    picked = (corner_ids[:, :, None] == table_ids[None, None, :]).astype(jnp.float32)
    blended = lax.optimization_barrier(jnp.sum(picked * corner_weights(pos_index.shape[1])[None, :, None], axis=1))
    use_blend = (long_rows == 1) & (offset >= 1)
    coeffs = jnp.where(use_blend[:, None], blended, direct) * valid.astype(jnp.float32)[:, None]
    return (segment, valid, coeffs)

def layer_norm(stream, gain_vec, shift_vec):
    row_mean = lax.optimization_barrier(jnp.mean(stream, axis=-1, keepdims=True))
    centered = stream - row_mean
    variance = lax.optimization_barrier(jnp.mean(centered * centered, axis=-1, keepdims=True))
    return centered * lax.rsqrt(variance + LN_EPSILON) * gain_vec + shift_vec

def attention_branch(normed, weights, bias_vec, bias_out_vec, same_image):
    model_width = normed.shape[1]
    row_count = normed.shape[0]
    qkv_bias = jnp.concatenate([bias_vec[:model_width], jnp.zeros((model_width,), jnp.float32), bias_vec[2 * model_width:3 * model_width]])
    qkv = low_back(low(jnp.dot(normed, weights[:, :3 * model_width], precision=FULL_PRECISION) + qkv_bias))
    queries = qkv[:, :model_width].reshape(row_count, HEADS, HEAD_DIM)
    key_rows = qkv[:, model_width:2 * model_width].reshape(row_count, HEADS, HEAD_DIM)
    values = qkv[:, 2 * model_width:].reshape(row_count, HEADS, HEAD_DIM)
    scores = low_back(jnp.einsum('qhd,khd->hqk', queries, key_rows, precision=FULL_PRECISION) * HEAD_DIM ** (-0.5))
    scores = jnp.where(same_image[None], scores, MASKED_SCORE)
    row_max = lax.optimization_barrier(jnp.max(scores, axis=-1, keepdims=True))
    exp_terms = jnp.exp(scores - row_max)
    attn_probs = low(exp_terms / lax.optimization_barrier(jnp.sum(exp_terms, axis=-1, keepdims=True)))
    mixed = jnp.einsum('hqk,khd->qhd', attn_probs, values, precision=FULL_PRECISION).reshape(row_count, model_width)
    mixed = low_back(low(mixed))
    return low_back(jnp.dot(mixed, weights[:, 3 * model_width:], precision=FULL_PRECISION) + bias_out_vec)

def feed_forward(normed, weights_in, bias_vec, weights_out, bias_out_vec):
    inner = low_back(jnp.dot(normed, weights_in, precision=FULL_PRECISION) + bias_vec)
    activated = low(jax.nn.gelu(inner, approximate=False))
    return low_back(jnp.dot(activated, weights_out, precision=FULL_PRECISION) + bias_out_vec)

def forward(param_set, table, token_block, segment, valid, coeffs):
    slab_in, slab_out, bias_in, bias_out, ln_gain, ln_bias = param_set
    stream = token_block + jnp.dot(coeffs, table, precision=FULL_PRECISION)
    keep_mask = valid.astype(jnp.float32)[:, None]
    same_image = segment[:, None] == segment[None, :]
    stream_sq = []
    branch_sq = []
    for sublayer in range(2 * LAYERS):
        normed = low(layer_norm(stream, ln_gain[sublayer], ln_bias[sublayer]))
        if sublayer % 2 == 0:
            branch = attention_branch(normed, slab_in[sublayer], bias_in[sublayer], bias_out[sublayer], same_image)
        else:
            branch = feed_forward(normed, slab_in[sublayer], bias_in[sublayer], slab_out[sublayer], bias_out[sublayer])
        stream = stream + branch
        stream_sq.append(jnp.sum(keep_mask * stream * stream))
        branch_sq.append(jnp.sum(keep_mask * branch * branch))
    return (stream, (jnp.stack(stream_sq), jnp.stack(branch_sq)))

def reference(inputs, cotangent, layout, pos_index, pos_table, slab_in, slab_out, bias_in, bias_out, ln_gain, ln_bias):
    params = tuple((weight_arr.astype(jnp.float32) for weight_arr in (slab_in, slab_out, bias_in, bias_out, ln_gain, ln_bias)))
    table = pos_table.astype(jnp.float32)
    buffer_count = inputs.shape[0] * (inputs.shape[1] // ROWS)
    model_width = inputs.shape[2]
    token_rows = inputs.reshape(buffer_count, ROWS, model_width)
    cot_rows = cotangent.reshape(buffer_count, ROWS, model_width)
    layout_rows = layout.reshape(buffer_count, layout.shape[2])
    zero_grads = tuple((jnp.zeros(weight_arr.shape, jnp.float32) for weight_arr in params))

    def one_buffer(scan_carry, buffer_item):
        grad_sums, pos_sum, square_sums, token_count = scan_carry
        token_block, cot_block, layout_row = buffer_item
        segment, valid, coeffs = tables(layout_row, pos_index, ROWS)

        def run_buffer(param_set, table_in, token_in):
            return forward(param_set, table_in, token_in, segment, valid, coeffs)
        result, back_fn, (stream_sq, branch_sq) = jax.vjp(run_buffer, params, table, token_block.astype(jnp.float32), has_aux=True)
        masked_cot = cot_block.astype(jnp.float32) * valid.astype(jnp.float32)[:, None]
        grad_params, grad_table, grad_tokens = back_fn(masked_cot)
        grad_sums = jax.tree.map(lambda running, addend: running + addend, grad_sums, grad_params)
        new_carry = (grad_sums, pos_sum + grad_table, square_sums + jnp.stack([stream_sq, branch_sq]), token_count + jnp.sum(valid.astype(jnp.float32)))
        return (new_carry, (result.astype(jnp.bfloat16), grad_tokens.astype(jnp.bfloat16)))
    initial = (zero_grads, jnp.zeros(table.shape, jnp.float32), jnp.zeros((2, 2 * LAYERS), jnp.float32), jnp.zeros((), jnp.float32))
    final_carry, (outputs, token_grads) = lax.scan(one_buffer, initial, (token_rows, cot_rows, layout_rows))
    grad_sums, pos_sum, square_sums, token_count = final_carry
    stats = jnp.sqrt(square_sums / (token_count * model_width))
    return (outputs.reshape(inputs.shape), token_grads.reshape(inputs.shape), grad_sums[0], grad_sums[1], grad_sums[2], grad_sums[3], grad_sums[4], grad_sums[5], pos_sum, stats)
```

```python
import functools

import jax
import jax.numpy as jnp
from jax import lax
from jax.experimental import pallas as pl
from jax.experimental.pallas import tpu as pltpu
from jax.sharding import PartitionSpec as P

BF = jnp.bfloat16
F32 = jnp.float32
I32 = jnp.int32
MESH = pl.DeviceIdType.MESH

D = 1024
FF = 4096
HEAD_DIM = 64
SHORT = 50
LONG = 145
MICRO = 4
ROWS = 160
ALL = MICRO * ROWS
SLOTS = 3
GROUP = 4
WIDE = GROUP * HEAD_DIM
KINDS = 256
TABLE = 128
LN_EPSILON = 1e-06
MASKED_SCORE = -1e30
INV_SQRT2 = 0.7071067811865476
INV_SQRT_2PI = 0.3989422804014327
MIB = 2**20


def dot(a, b):
    return lax.dot_general(a, b, (((1,), (0,)), ((), ())), preferred_element_type=F32)


def dot_nt(a, b):
    return lax.dot_general(a, b, (((1,), (1,)), ((), ())), preferred_element_type=F32)


def dot_tn(a, b):
    return lax.dot_general(a, b, (((0,), (0,)), ((), ())), preferred_element_type=F32)


def split(v):
    high = v.astype(BF)
    return high, (v - high.astype(F32)).astype(BF)


def col_sum(v):
    return jnp.sum(v, axis=0, keepdims=True)


def pipeline_kernel(
    lay, inp, cot, slab_in, slab_out, bi, bo, ga, sh, blend, table,
    a1_o, g1_o, a2_o, g2_o, edge_o, small_o, pos_o,
    w_in, w_out, w_in_t, w_out_t, xs, ds, xo, do, a1, g1, a2, xhat, rstd, xf, vec_in, vec,
    pos_hi, pos_lo, gpos,
    load_sem, f_send, f_recv, b_send, b_recv, out_sem,
):
    sec = lax.axis_index("section")
    is_att = sec % 2 == 0
    first = sec == 0
    last = sec == 3
    left = {"section": lax.rem(sec + 3, 4)}
    right = {"section": lax.rem(sec + 1, 4)}

    load_in = pltpu.make_async_copy(slab_in.at[0], w_in, load_sem.at[0])
    load_out = pltpu.make_async_copy(slab_out.at[0], w_out, load_sem.at[1])
    load_x = pltpu.make_async_copy(inp, xs, load_sem.at[2])
    load_d = pltpu.make_async_copy(cot, ds, load_sem.at[3])

    @pl.when(first)
    def _():
        load_x.start()

    load_in.start()

    @pl.when(jnp.logical_not(is_att))
    def _():
        load_out.start()

    @pl.when(last)
    def _():
        load_d.start()

    barrier = pltpu.get_barrier_semaphore()

    @pl.when(sec > 0)
    def _():
        pl.semaphore_signal(barrier, inc=1, device_id=left, device_id_type=MESH)

    @pl.when(sec < 3)
    def _():
        pl.semaphore_signal(barrier, inc=1, device_id=right, device_id_type=MESH)

    @pl.when(first | last)
    def _():
        pl.semaphore_wait(barrier, 1)

    @pl.when(jnp.logical_not(first | last))
    def _():
        pl.semaphore_wait(barrier, 2)

    def forward_copy(m):
        return pltpu.make_async_remote_copy(
            src_ref=xo.at[m], dst_ref=xs.at[m], send_sem=f_send.at[m], recv_sem=f_recv.at[m],
            device_id=right, device_id_type=MESH)

    def backward_copy(m):
        return pltpu.make_async_remote_copy(
            src_ref=do.at[m], dst_ref=ds.at[m], send_sem=b_send.at[m], recv_sem=b_recv.at[m],
            device_id=left, device_id_type=MESH)

    def rows_of(m):
        return pl.ds(pl.multiple_of(m * ROWS, ROWS), ROWS)

    def save(kind, m, src, dst):
        return pltpu.make_async_copy(src, dst, out_sem.at[kind, m])

    def save_a1(m):
        return save(0, m, a1.at[rows_of(m)], a1_o.at[rows_of(m)])

    def save_g1(m):
        return save(1, m, g1.at[rows_of(m)], g1_o.at[rows_of(m)])

    def save_a2(m):
        return save(2, m, a2.at[rows_of(m)], a2_o.at[rows_of(m)])

    def save_mixed(m):
        return save(2, m, a2.at[rows_of(m), 0:D], a2_o.at[rows_of(m), 0:D])

    def save_g2(m):
        return save(3, m, ds.at[m], g2_o.at[rows_of(m)])

    def save_last(m):
        return save(4, m, xo.at[m], edge_o.at[m])

    def save_first(m):
        return save(4, m, do.at[m], edge_o.at[m])

    vec_in[...] = jnp.zeros_like(vec_in)
    vec[...] = jnp.zeros_like(vec)
    gain = ga[...].astype(F32)
    shift = sh[...].astype(F32)
    bias_out = bo[...].astype(F32)

    def ends_of(m):
        ends, total = [], jnp.int32(0)
        for k in range(SLOTS):
            kind = lay[m, k]
            total = total + jnp.where(kind == 1, SHORT, jnp.where(kind == 2, LONG, 0))
            ends.append(total)
        return ends

    def segment(ends, ids):
        return jnp.where(
            ids < ends[0], 0, jnp.where(ids < ends[1], 1, jnp.where(ids < ends[2], 2, -1)))

    def keep_of(m):
        ends = ends_of(m)
        return (lax.broadcasted_iota(I32, (ROWS, 1), 0) < ends[2]).astype(F32)

    def places(m):
        ends = ends_of(m)
        ids = lax.broadcasted_iota(I32, (ROWS, 1), 0)
        starts = [jnp.int32(0), ends[0], ends[1]]
        place = jnp.full((ROWS, 1), -1, I32)
        for k in range(SLOTS):
            base = jnp.where(lay[m, k] == 1, LONG, 0)
            place = jnp.where((ids >= starts[k]) & (ids < ends[k]), ids - starts[k] + base, place)
        return (place == lax.broadcasted_iota(I32, (ROWS, KINDS), 1)).astype(F32).astype(BF)

    def norm(rows, x):
        mean = jnp.mean(x, axis=1, keepdims=True)
        centered = x - mean
        variance = jnp.mean(centered * centered, axis=1, keepdims=True)
        scale = lax.rsqrt(variance + LN_EPSILON)
        hat = centered * scale
        rstd[rows, :] = scale
        xhat[rows, :] = hat.astype(BF)
        a1[rows, :] = (hat * gain + shift).astype(BF)

    def norm_back(rows, d_normed, d):
        hat = xhat[rows, :].astype(F32)
        vec[1:2, :] += col_sum(d_normed * hat)
        vec[2:3, :] += col_sum(d_normed)
        e = gain * d_normed
        mean_e = jnp.mean(e, axis=1, keepdims=True)
        mean_eh = jnp.mean(e * hat, axis=1, keepdims=True)
        return d + rstd[rows, :] * (e - mean_e - hat * mean_eh)

    def finish_forward(m, x, branch):
        out = x + branch
        keep = keep_of(m)
        vec[3:4, :] += col_sum(keep * out * out)
        vec[4:5, :] += col_sum(keep * branch * branch)
        xo[m] = out.astype(BF)

        @pl.when(sec < 3)
        def _():
            forward_copy(m).start()

        @pl.when(last)
        def _():
            save_last(m).start()

    def finish_backward(m, d_prev):
        do[m] = d_prev.astype(BF)

        @pl.when(sec > 0)
        def _():
            backward_copy(m).start()

        @pl.when(first)
        def _():
            save_first(m).start()

    def transpose_in():
        def step(i, carry):
            cols = pl.ds(pl.multiple_of(i * 256, 256), 256)
            w_in_t[cols, :] = w_in[:, cols].T
            return carry

        lax.fori_loop(0, FF // 256, step, 0)

    def transpose_out():
        def step(i, carry):
            cols = pl.ds(pl.multiple_of(i * 256, 256), 256)
            w_out_t[:, cols] = w_out[cols, :].T
            return carry

        lax.fori_loop(0, FF // 256, step, 0)

    lane_head = lax.broadcasted_iota(I32, (1, WIDE), 1) // HEAD_DIM
    masks = [(lane_head == h).astype(F32) for h in range(GROUP)]
    masks_low = [m.astype(BF) for m in masks]

    def spread(v):
        return jnp.concatenate([v * mask for mask in masks_low], axis=0)

    def gather_heads(v):
        v = v.reshape(GROUP, ROWS, WIDE)
        return v[0] * masks[0] + v[1] * masks[1] + v[2] * masks[2] + v[3] * masks[3]

    def probs_at(m, g):
        return w_out.at[pl.ds(pl.multiple_of(m * 640, 640), 640), g * WIDE:g * WIDE + ROWS]

    def attention_forward(m):
        rows = rows_of(m)

        @pl.when(sec > 0)
        def _():
            forward_copy(m).wait_recv()

        xf[...] = xs[m].astype(F32)

        @pl.when(first)
        def _():
            hot = places(m)
            xf[...] += dot(hot, pos_hi[...]) + dot(hot, pos_lo[...])

        norm(rows, xf[...])
        save_a1(m).start()
        for part in range(3):
            cols = slice(part * D, (part + 1) * D)
            proj = dot(a1[rows, :], w_in[:, cols])
            if part != 1:
                proj = proj + bi[:, cols].astype(F32)
            a2[rows, (part + 1) * D:(part + 2) * D] = proj.astype(BF)
        ends = ends_of(m)
        seg_rows = segment(ends, lax.broadcasted_iota(I32, (ROWS, ROWS), 0))
        seg_cols = segment(ends, lax.broadcasted_iota(I32, (ROWS, ROWS), 1))
        same = seg_rows == seg_cols
        for g in range(D // WIDE):
            lo = D + g * WIDE
            q = spread(a2[rows, lo:lo + WIDE])
            k = a2[rows, D + lo:D + lo + WIDE]
            v = a2[rows, 2 * D + lo:2 * D + lo + WIDE]
            s = dot_nt(q, k).reshape(GROUP, ROWS, ROWS) * HEAD_DIM ** (-0.5)
            s = jnp.where(same[None], s, MASKED_SCORE)
            s = jnp.exp(s - jnp.max(s, axis=2, keepdims=True))
            p = s * (1.0 / jnp.sum(s, axis=2, keepdims=True))
            p = p.reshape(GROUP * ROWS, ROWS).astype(BF)
            probs_at(m, g)[...] = p
            a2[rows, g * WIDE:(g + 1) * WIDE] = gather_heads(dot(p, v)).astype(BF)
        save_mixed(m).start()
        branch = dot(a2[rows, 0:D], w_in[:, 3 * D:4 * D]) + bias_out
        finish_forward(m, xf[...], branch)

    def attention_backward(m):
        rows = rows_of(m)
        backward_copy(m).wait_recv()
        save_g2(m).start()
        d = ds[m]
        vec[0:1, :] += col_sum(d.astype(F32))
        d_mixed = dot(d, w_in_t[3 * D:4 * D, :]).astype(BF)
        for g in range(D // WIDE):
            lo = D + g * WIDE
            q = spread(a2[rows, lo:lo + WIDE])
            k = a2[rows, D + lo:D + lo + WIDE]
            v = a2[rows, 2 * D + lo:2 * D + lo + WIDE]
            dm = spread(d_mixed[:, g * WIDE:(g + 1) * WIDE])
            p = probs_at(m, g)[...]
            dp = dot_nt(dm, v)
            pf = p.astype(F32)
            row_dot = jnp.sum(pf * dp, axis=1, keepdims=True)
            d_s = (pf * (dp - row_dot)).astype(BF)
            dq = (gather_heads(dot(d_s, k)) * HEAD_DIM ** (-0.5)).astype(BF)
            dk = (dot_tn(d_s, q) * HEAD_DIM ** (-0.5)).astype(BF)
            dv = dot_tn(p, dm).astype(BF)
            gs = slice(g * WIDE, (g + 1) * WIDE)
            vs = slice(2 * D + g * WIDE, 2 * D + (g + 1) * WIDE)
            g1[rows, gs] = dq
            g1[rows, D + g * WIDE:D + (g + 1) * WIDE] = dk
            g1[rows, vs] = dv
            vec_in[0:1, gs] += col_sum(dq.astype(F32))
            vec_in[0:1, vs] += col_sum(dv.astype(F32))
        save_g1(m).start()
        d_normed = dot(g1[rows, 0:3 * D], w_in_t[0:3 * D, :])
        d_prev = norm_back(rows, d_normed, d.astype(F32))
        finish_backward(m, d_prev)

        @pl.when(first)
        def _():
            gpos[...] += dot_tn(places(m), do[m])

    def feed_forward(m):
        rows = rows_of(m)
        forward_copy(m).wait_recv()
        x = xs[m].astype(F32)
        norm(rows, x)
        save_a1(m).start()
        for part in range(4):
            cols = slice(part * D, (part + 1) * D)
            v = dot(a1[rows, :], w_in[:, cols]) + bi[:, cols].astype(F32)
            cdf = 0.5 + 0.5 * lax.erf(v * INV_SQRT2)
            a2[rows, cols] = (v * cdf).astype(BF)
            g1[rows, cols] = (cdf + v * (INV_SQRT_2PI * jnp.exp(-0.5 * v * v))).astype(BF)
        save_a2(m).start()
        branch = dot(a2[rows, :], w_out[...]) + bias_out
        finish_forward(m, xs[m].astype(F32), branch)

    def feed_backward(m):
        rows = rows_of(m)

        @pl.when(sec < 3)
        def _():
            backward_copy(m).wait_recv()

        @pl.when(last)
        def _():
            ds[m] = (ds[m].astype(F32) * keep_of(m)).astype(BF)

        save_g2(m).start()
        d = ds[m]
        vec[0:1, :] += col_sum(d.astype(F32))
        for part in range(4):
            cols = slice(part * D, (part + 1) * D)
            d_inner = (dot(d, w_out_t[:, cols]) * g1[rows, cols].astype(F32)).astype(BF)
            g1[rows, cols] = d_inner
            vec_in[0:1, cols] += col_sum(d_inner.astype(F32))
        save_g1(m).start()
        d_normed = dot(g1[rows, :], w_in_t[...])
        finish_backward(m, norm_back(rows, d_normed, d.astype(F32)))

    @pl.when(is_att)
    def _():
        @pl.when(first)
        def _():
            high, low = split(blend[...])
            rows = dot(high, table[...]) + dot(low, table[...])
            pos_hi[...], pos_lo[...] = split(rows)
            gpos[...] = jnp.zeros_like(gpos)
            load_x.wait()

        load_in.wait()

        @pl.when(sec > 0)
        def _():
            transpose_in()

        def fwd(m, carry):
            attention_forward(m)
            return carry

        lax.fori_loop(0, MICRO, fwd, 0)

        @pl.when(first)
        def _():
            transpose_in()

        def bwd(m, carry):
            attention_backward(m)
            return carry

        lax.fori_loop(0, MICRO, bwd, 0)

    @pl.when(jnp.logical_not(is_att))
    def _():
        load_in.wait()
        load_out.wait()

        @pl.when(last)
        def _():
            load_d.wait()

        def tick(t, carry):
            @pl.when((last & (t == 0)) | (jnp.logical_not(last) & (t == MICRO)))
            def _():
                transpose_out()
                transpose_in()

            is_fwd = (last & (t % 2 == 0)) | (jnp.logical_not(last) & (t < MICRO))
            m = jnp.where(last, t // 2, t % MICRO)

            @pl.when(is_fwd)
            def _():
                feed_forward(m)

            @pl.when(jnp.logical_not(is_fwd))
            def _():
                feed_backward(m)

            return carry

        lax.fori_loop(0, 2 * MICRO, tick, 0)

    count = jnp.int32(0)
    for m in range(MICRO):
        count = count + ends_of(m)[2]
    lanes = lax.broadcasted_iota(I32, (1, 128), 1)
    stream_sq = jnp.sum(vec[3:4, :], axis=1, keepdims=True)
    branch_sq = jnp.sum(vec[4:5, :], axis=1, keepdims=True)
    stat = jnp.where(
        lanes == 0, stream_sq,
        jnp.where(lanes == 1, branch_sq, jnp.where(lanes == 2, count.astype(F32), 0.0)))
    small_o[...] = jnp.zeros_like(small_o)
    for j in range(32):
        quad = slice((j // 4) * 128, (j // 4 + 1) * 128)
        small_o[j, 0:1, :] = vec_in[0:1, j * 128:(j + 1) * 128]
        small_o[j, 1:4, :] = vec[0:3, quad]
        small_o[j, 4:5, :] = stat

    @pl.when(first)
    def _():
        g_hi, g_lo = split(gpos[...])
        b_hi, b_lo = split(blend[...])
        pos_o[...] = dot_tn(g_hi, b_hi) + dot_tn(g_lo, b_hi) + dot_tn(g_hi, b_lo)

    @pl.when(sec > 0)
    def _():
        pos_o[...] = jnp.zeros_like(pos_o)

    def drain(m, carry):
        save_a1(m).wait()
        save_g1(m).wait()
        save_g2(m).wait()

        @pl.when(is_att)
        def _():
            save_mixed(m).wait()

        @pl.when(jnp.logical_not(is_att))
        def _():
            save_a2(m).wait()

        @pl.when(last)
        def _():
            save_last(m).wait()

        @pl.when(first)
        def _():
            save_first(m).wait()

        @pl.when(sec < 3)
        def _():
            forward_copy(m).wait_send()

        @pl.when(sec > 0)
        def _():
            backward_copy(m).wait_send()

        return carry

    lax.fori_loop(0, MICRO, drain, 0)


def reduce_kernel(
    a1_h, g1_h, a2_h, g2_h, edge, small, pos,
    layer_o, input_o, gin_o, gout_o, small_out, stats_o, gpos_o,
    a1, g1, a2, g2, grad, cross, ring1, ring2, layer_s, input_s,
    sm_x, sm_acc, sm_z, sm_acc2, sm_y, ps_x, ps_acc, ps_z, ps_acc2, ps_y, pos_tile, stat_s, pos_s,
    load_sem, c_send, c_recv, s1_send, s1_recv, s2_send, s2_recv,
    sm_send, sm_recv, ps_send, ps_recv, x_send, x_recv, e_send, e_recv, own_sem,
):
    sec = lax.axis_index("section")
    dp = lax.axis_index("dp")
    z, y, c = dp // 8, (dp // 2) % 4, dp % 2
    other = 1 - c
    is_att = sec % 2 == 0

    def at_dp(zz, yy, cc):
        return {"dp": (zz * 4 + yy) * 2 + cc}

    def plus(v, k):
        return lax.rem(v + k, 4)

    sibling = at_dp(z, y, other)
    z_peers = {k: at_dp(plus(z, k), y, c) for k in (1, 2, 3)}
    y_peers = {k: at_dp(z, plus(y, k), c) for k in (1, 2, 3)}
    x_peers = {k: {"section": plus(sec, k)} for k in (1, 2, 3)}

    loads = [
        pltpu.make_async_copy(src, dst, load_sem.at[i])
        for i, (src, dst) in enumerate(((a1_h, a1), (g1_h, g1), (a2_h, a2), (g2_h, g2)))
    ]
    for load in loads:
        load.start()

    barrier = pltpu.get_barrier_semaphore()
    partners = [sibling] + [z_peers[k] for k in (1, 2, 3)] + [y_peers[k] for k in (1, 2, 3)]
    partners += [x_peers[k] for k in (1, 2, 3)]
    for partner in partners:
        pl.semaphore_signal(barrier, inc=1, device_id=partner, device_id_type=MESH)
    pl.semaphore_wait(barrier, len(partners))

    def remote(src, dst, send, recv, device):
        return pltpu.make_async_remote_copy(
            src_ref=src, dst_ref=dst, send_sem=send, recv_sem=recv, device_id=device,
            device_id_type=MESH)

    def columns(s):
        return edge.at[:, :, pl.ds(pl.multiple_of(s * 256, 256), 256)]

    def edge_copy(k, landing, kind):
        return remote(columns(plus(sec, k)), landing, e_send.at[k - 1], e_recv.at[kind],
                      x_peers[k])

    @pl.when(sec == 3)
    def _():
        for k in (1, 2, 3):
            edge_copy(k, layer_s, 0).start()
        pltpu.make_async_copy(columns(3), layer_s, own_sem.at[0]).start()

    @pl.when(sec == 0)
    def _():
        for k in (1, 2, 3):
            edge_copy(k, input_s, 1).start()
        pltpu.make_async_copy(columns(0), input_s, own_sem.at[0]).start()

    for load in loads:
        load.wait()

    def reduce(height, make):
        half = height // 2
        coords = ((z, y), (y, z))
        peers = ((z_peers, y_peers), (y_peers, z_peers))

        def chunk(core, s, a):
            return grad.at[core, s, a, :, 0:height, :]

        def cross_copy(s, a):
            return remote(chunk(other, s, a), cross.at[s, a, :, 0:height, :], c_send.at[s, a],
                          c_recv.at[s, a], sibling)

        def first_half(s, a, h):
            return grad.at[c, s, a, 2 * h:2 * h + 2, 0:height, :]

        def landing1(s, i):
            return ring1.at[s, i, :, 0:height, :]

        def step1(s, i):
            p1 = coords[s][0]
            a, h = {0: (plus(p1, 2), 0), 1: (plus(p1, 2), 1), 2: (plus(p1, 1), 1),
                    3: (plus(p1, 3), 0), 4: (plus(p1, 1), 0), 5: (plus(p1, 3), 1)}[i]
            peer = peers[s][0][1 if i % 2 == 0 else 3]
            return remote(first_half(s, a, h), landing1(s, i), s1_send.at[s, i], s1_recv.at[s, i],
                          peer)

        def second_half(s, b, h):
            return grad.at[c, s, coords[s][0], b, h * half:(h + 1) * half, :]

        def landing2(s, i):
            return ring2.at[s, i, 0:half, :]

        def step2(s, i):
            p2 = coords[s][1]
            b, h = {0: (plus(p2, 2), 0), 1: (plus(p2, 2), 1), 2: (plus(p2, 1), 1),
                    3: (plus(p2, 3), 0), 4: (plus(p2, 1), 0), 5: (plus(p2, 3), 1)}[i]
            peer = peers[s][1][1 if i % 2 == 0 else 3]
            return remote(second_half(s, b, h), landing2(s, i), s2_send.at[s, i],
                          s2_recv.at[s, i], peer)

        def join(s, a):
            cross_copy(s, a).wait_recv()

            def add(b, carry):
                mine = grad.at[c, s, a, b, 0:height, :]
                mine[...] = mine[...] + cross[s, a, b, 0:height, :]
                return carry

            lax.fori_loop(0, 4, add, 0)

        order = (2, 1, 3, 0)

        def arrived(n):
            for s in (0, 1):
                p1 = coords[s][0]
                join(s, plus(p1, order[n]))
                for i in {0: (0, 1), 1: (2,), 2: (3,), 3: ()}[n]:
                    step1(s, i).start()

        for n in range(4):
            for s in (0, 1):
                a = plus(coords[s][0], order[n])
                make(s, a, n)
                cross_copy(s, a).start()
            if n > 0:
                arrived(n - 1)
        arrived(3)
        for s in (0, 1):
            p1 = coords[s][0]
            for i, a, h in ((4, plus(p1, 1), 0), (5, plus(p1, 3), 1)):
                step1(s, i - 4).wait_recv()
                for q in range(2):
                    part = grad.at[c, s, a, 2 * h + q, 0:height, :]
                    part[...] = part[...] + ring1[s, i - 4, q, 0:height, :]
                step1(s, i).start()
        small_work = small_reduce()
        for s in (0, 1):
            p1 = coords[s][0]
            for i in (2, 3, 4, 5):
                step1(s, i).wait_recv()
            p2 = coords[s][1]
            for n in order:
                b = plus(p2, n)
                row = grad.at[c, s, p1, b, 0:height, :]
                h = b // 2
                q = b % 2
                up = ring1[s, jnp.where(h == 0, 4, 2), q, 0:height, :].astype(F32)
                down = ring1[s, jnp.where(h == 0, 3, 5), q, 0:height, :].astype(F32)
                row[...] = (row[...].astype(F32) + up + down).astype(BF)
                for i in {2: (0, 1), 1: (2,), 3: (3,), 0: ()}[n]:
                    step2(s, i).start()
        for s in (0, 1):
            p2 = coords[s][1]
            for i, b, h in ((4, plus(p2, 1), 0), (5, plus(p2, 3), 1)):
                step2(s, i - 4).wait_recv()
                part = second_half(s, b, h)
                part[...] = part[...] + ring2[s, i - 4, 0:half, :]
                step2(s, i).start()
        results = []
        for s in (0, 1):
            for i in (2, 3, 4, 5):
                step2(s, i).wait_recv()
            p2 = coords[s][1]
            low = second_half(s, p2, 0)[...].astype(F32)
            low = low + ring2[s, 4, 0:half, :].astype(F32) + ring2[s, 3, 0:half, :].astype(F32)
            high = second_half(s, p2, 1)[...].astype(F32)
            high = high + ring2[s, 2, 0:half, :].astype(F32) + ring2[s, 5, 0:half, :].astype(F32)
            results.append(jnp.concatenate([low, high], axis=0))
        for s in (0, 1):
            for a in range(4):
                cross_copy(s, a).wait_send()
            for i in range(6):
                step1(s, i).wait_send()
                step2(s, i).wait_send()
        return results

    def tiny_reduce(src, got_x, acc, got_z, acc2, got_y, send, recv):
        def cross_tiny():
            return remote(src.at[:, :, other], got_x, send.at[0], recv.at[0], sibling)

        def z_tiny(k):
            return remote(acc.at[plus(z, k)], got_z.at[k - 1], send.at[k], recv.at[k], z_peers[k])

        def y_tiny(k):
            return remote(acc2.at[plus(y, k)], got_y.at[k - 1], send.at[3 + k], recv.at[3 + k],
                          y_peers[k])

        cross_tiny().start()
        cross_tiny().wait_recv()
        acc[...] = src[:, :, c] + got_x[...]
        for k in (1, 2, 3):
            z_tiny(k).start()
        for k in (1, 2, 3):
            z_tiny(k).wait_recv()
        acc2[...] = acc[z] + got_z[0] + got_z[1] + got_z[2]
        for k in (1, 2, 3):
            y_tiny(k).start()
        for k in (1, 2, 3):
            y_tiny(k).wait_recv()
        total = acc2[y] + got_y[0] + got_y[1] + got_y[2]
        cross_tiny().wait_send()
        for k in (1, 2, 3):
            z_tiny(k).wait_send()
            y_tiny(k).wait_send()
        return total

    def small_reduce():
        small_out[...] = tiny_reduce(small, sm_x, sm_acc, sm_z, sm_acc2, sm_y, sm_send, sm_recv)

    def lhs(ref, start, width):
        return ref[:, pl.ds(pl.multiple_of(start, width), width)].T

    @pl.when(jnp.logical_not(is_att))
    def _():
        def make(s, a, n):
            if s == 0:
                left = lhs(a1, a * 256, 256)
                for cb in range(4):
                    block = dot(left, g1[:, cb * D:(cb + 1) * D]).astype(BF)
                    for yy in range(4):
                        for cc in range(2):
                            at = yy * 64 + cc * 32
                            grad[cc, 0, a, yy, cb * 32:(cb + 1) * 32, :] = block[at:at + 32, :]
            else:
                def step(zz, carry):
                    block = dot(lhs(a2, zz * 1024 + a * 256, 256), g2[...]).astype(BF)
                    for cc in range(2):
                        grad[cc, 1, a, zz, :, :] = block[cc * 128:(cc + 1) * 128, :]
                    return carry

                lax.fori_loop(0, 4, step, 0)

        first, second = reduce(128, make)
        for cb in range(4):
            gin_o[:, cb * D:(cb + 1) * D] = first[cb * 32:(cb + 1) * 32, :]
        gout_o[...] = second

    @pl.when(is_att)
    def _():
        def make(s, a, n):
            if s == 0:
                left = lhs(a1, a * 256, 256)
                for cb in range(2):
                    block = dot(left, g1[:, cb * D:(cb + 1) * D]).astype(BF)
                    for yy in range(4):
                        for cc in range(2):
                            at = yy * 64 + cc * 32
                            grad[cc, 0, a, yy, cb * 32:(cb + 1) * 32, :] = block[at:at + 32, :]
            elif n == 0:
                def step(zz, carry):
                    for cb in range(2):
                        if cb == 0:
                            block = dot(lhs(a1, zz * 256, 256), g1[:, 2 * D:3 * D]).astype(BF)
                        else:
                            block = dot(lhs(a2, zz * 256, 256), g2[...]).astype(BF)
                        for yy in range(4):
                            for cc in range(2):
                                at = yy * 64 + cc * 32
                                grad[cc, 1, yy, zz, cb * 32:(cb + 1) * 32, :] = block[at:at + 32, :]
                    return carry

                lax.fori_loop(0, 4, step, 0)

        first, second = reduce(64, make)
        for cb in range(2):
            gin_o[:, cb * D:(cb + 1) * D] = first[cb * 32:(cb + 1) * 32, :]
            gin_o[:, (2 + cb) * D:(3 + cb) * D] = second[cb * 32:(cb + 1) * 32, :]
        gout_o[...] = jnp.zeros_like(gout_o)
        pos_tile[...] = tiny_reduce(pos, ps_x, ps_acc, ps_z, ps_acc2, ps_y, ps_send, ps_recv)

    def stat_copy(k):
        return remote(small_out, stat_s.at[sec], x_send.at[k - 1], x_recv.at[k - 1], x_peers[k])

    def pos_copy(k):
        return remote(pos_tile.at[k], pos_s, x_send.at[2 + k], x_recv.at[3], x_peers[k])

    for k in (1, 2, 3):
        stat_copy(k).start()

    @pl.when(sec == 0)
    def _():
        for k in (1, 2, 3):
            pos_copy(k).start()
        pos_s[...] = pos_tile[0]
        pltpu.make_async_copy(columns(0), input_s, own_sem.at[0]).wait()
        edge_copy(1, layer_s, 0).wait_recv()

    @pl.when(sec > 0)
    def _():
        edge_copy(1, input_s, 1).wait_recv()

        @pl.when(sec < 3)
        def _():
            edge_copy(1, layer_s, 0).wait_recv()

        @pl.when(sec == 3)
        def _():
            pltpu.make_async_copy(columns(3), layer_s, own_sem.at[0]).wait()

        pos_copy(1).wait_recv()

    stat_s[sec] = small_out[...]
    for k in (1, 2, 3):
        stat_copy(k).wait_recv()
    stats_o[...] = stat_s[...]
    gpos_o[...] = pos_s[...]
    layer_o[...] = layer_s[...]
    input_o[...] = input_s[...]

    for k in (1, 2, 3):
        stat_copy(k).wait_send()

    @pl.when(sec == 0)
    def _():
        for k in (1, 2, 3):
            pos_copy(k).wait_send()
            edge_copy(k, input_s, 1).wait_send()

    @pl.when(sec == 3)
    def _():
        for k in (1, 2, 3):
            edge_copy(k, layer_s, 0).wait_send()


def blend_matrix(pos_index):
    corners = pos_index.shape[1]
    weights = (corners - jnp.arange(corners, dtype=F32)) / (corners * (corners + 1) / 2.0)
    ids = jnp.pad(pos_index, ((1, KINDS - LONG), (0, 0)), constant_values=-1)
    columns = jnp.arange(TABLE, dtype=I32)
    picked = (ids[:, :, None] == columns[None, None, :]).astype(F32)
    blended = jnp.sum(picked * weights[None, :, None], axis=1)
    rows = jnp.arange(KINDS, dtype=I32)[:, None]
    direct = jnp.where(rows >= LONG, rows - LONG, jnp.where(rows == 0, 0, -1))
    one = (direct == columns[None, :]) & (columns[None, :] < SHORT)
    return blended + one.astype(F32)


def local(inputs, cotangent, layout, pos_index, pos_table, slab_in, slab_out, bias_in, bias_out,
          ln_gain, ln_bias):
    shape = jax.ShapeDtypeStruct
    vmem = pl.BlockSpec(memory_space=pltpu.VMEM)
    smem = pl.BlockSpec(memory_space=pltpu.SMEM)
    anywhere = pl.BlockSpec(memory_space=pl.ANY)
    dma = pltpu.SemaphoreType.DMA

    blend = blend_matrix(pos_index)
    table = jnp.pad(pos_table, ((0, TABLE - SHORT), (0, 0)))
    a1, g1, a2, g2, edge, small, pos = pl.pallas_call(
        pipeline_kernel,
        name="pipeline",
        out_shape=(
            shape((ALL, D), BF), shape((ALL, FF), BF), shape((ALL, FF), BF), shape((ALL, D), BF),
            shape((MICRO, ROWS, D), BF), shape((32, 8, 128), F32), shape((D, TABLE), F32)),
        in_specs=[smem] + [anywhere] * 4 + [vmem] * 6,
        out_specs=(anywhere,) * 5 + (vmem,) * 2,
        scratch_shapes=[
            pltpu.VMEM((D, FF), BF), pltpu.VMEM((FF, D), BF),
            pltpu.VMEM((FF, D), BF), pltpu.VMEM((D, FF), BF),
            pltpu.VMEM((MICRO, ROWS, D), BF), pltpu.VMEM((MICRO, ROWS, D), BF),
            pltpu.VMEM((MICRO, ROWS, D), BF), pltpu.VMEM((MICRO, ROWS, D), BF),
            pltpu.VMEM((ALL, D), BF), pltpu.VMEM((ALL, FF), BF), pltpu.VMEM((ALL, FF), BF),
            pltpu.VMEM((ALL, D), BF), pltpu.VMEM((ALL, 1), F32), pltpu.VMEM((ROWS, D), F32),
            pltpu.VMEM((8, FF), F32), pltpu.VMEM((8, D), F32),
            pltpu.VMEM((KINDS, D), BF), pltpu.VMEM((KINDS, D), BF), pltpu.VMEM((KINDS, D), F32),
            dma((4,)), dma((MICRO,)), dma((MICRO,)), dma((MICRO,)), dma((MICRO,)),
            dma((5, MICRO)),
        ],
        compiler_params=pltpu.CompilerParams(
            collective_id=0, has_side_effects=True, vmem_limit_bytes=62 * MIB),
    )(layout[:, 0, :], inputs, cotangent, slab_in, slab_out, bias_in, bias_out, ln_gain, ln_bias,
      blend, table)

    small = small.reshape(4, 4, 2, 8, 128)
    pos = pos.reshape(4, 4, 4, 2, 8, 128).transpose(1, 2, 3, 0, 4, 5)

    def tiny(*tail):
        return [
            pltpu.VMEM((4, 4) + tail, F32), pltpu.VMEM((4, 4) + tail, F32),
            pltpu.VMEM((3, 4) + tail, F32), pltpu.VMEM((4,) + tail, F32),
            pltpu.VMEM((3,) + tail, F32)]

    layer_out, input_grad, grad_in, grad_out, own, stats, gpos = pl.pallas_call(
        reduce_kernel,
        name="reduce",
        out_shape=(
            shape((MICRO, ROWS, 256), BF), shape((MICRO, ROWS, 256), BF),
            shape((32, FF), F32), shape((128, D), F32), shape((8, 128), F32),
            shape((4, 8, 128), F32), shape((8, 128), F32)),
        in_specs=[anywhere] * 5 + [vmem] * 2,
        out_specs=(vmem,) * 7,
        scratch_shapes=[
            pltpu.VMEM((ALL, D), BF), pltpu.VMEM((ALL, FF), BF), pltpu.VMEM((ALL, FF), BF),
            pltpu.VMEM((ALL, D), BF),
            pltpu.VMEM((2, 2, 4, 4, 128, D), BF), pltpu.VMEM((2, 4, 4, 128, D), BF),
            pltpu.VMEM((2, 6, 2, 128, D), BF), pltpu.VMEM((2, 6, 64, D), BF),
            pltpu.VMEM((MICRO, ROWS, 256), BF), pltpu.VMEM((MICRO, ROWS, 256), BF),
            *tiny(8, 128), *tiny(4, 8, 128),
            pltpu.VMEM((4, 8, 128), F32), pltpu.VMEM((4, 8, 128), F32), pltpu.VMEM((8, 128), F32),
            dma((4,)), dma((2, 4)), dma((2, 4)), dma((2, 6)), dma((2, 6)), dma((2, 6)),
            dma((2, 6)), dma((7,)), dma((7,)), dma((7,)), dma((7,)), dma((6,)), dma((4,)),
            dma((3,)), dma((2,)), dma((1,)),
        ],
        compiler_params=pltpu.CompilerParams(
            collective_id=1, has_side_effects=True, vmem_limit_bytes=62 * MIB),
    )(a1, g1, a2, g2, edge, small, pos)

    quarter = lax.axis_index("dp") % 4
    vectors = lax.dynamic_index_in_dim(own[1:4].reshape(3, 4, 32), quarter, 1, keepdims=False)
    totals = stats[:, 4, :]
    stats_out = jnp.sqrt(totals[:, 0:2].T / (totals[0, 2] * D))
    return (
        layer_out, input_grad, grad_in[None], grad_out[None], own[0:1], vectors[0:1],
        vectors[1:2], vectors[2:3], gpos[:, 0:SHORT].T, stats_out)


def solution(mesh):
    return jax.shard_map(
        local,
        mesh=mesh,
        in_specs=(
            P(None, "dp", None), P(None, "dp", None), P(None, "dp", None), P(), P(),
            P("section", None, None), P("section", None, None), P("section", None),
            P("section", None), P("section", None), P("section", None)),
        out_specs=(
            P(None, "dp", "section"), P(None, "dp", "section"), P("section", "dp", None),
            P("section", "dp", None), P("section", "dp"), P("section", "dp"),
            P("section", "dp"), P("section", "dp"), P(None, ("section", "dp")), P()),
        check_vma=False,
    )
```

```python
import jax
import jax.numpy as jnp
from jax import lax
from jax.experimental import pallas as pl
from jax.experimental.pallas import tpu as pltpu
from jax.sharding import PartitionSpec as P

BF = jnp.bfloat16
F32 = jnp.float32
I32 = jnp.int32
MESH = pl.DeviceIdType.MESH

D = 1024
FF = 4096
HALF = FF // 2
HEAD_DIM = 64
SHORT = 50
LONG = 145
MICRO = 4
ROWS = 160
ALL = MICRO * ROWS
SLOTS = 3
GROUP = 4
WIDE = GROUP * HEAD_DIM
KINDS = 256
CORNERS = 4
LN_EPSILON = 1e-06
MASKED_SCORE = -1e30
INV_SQRT2 = 0.7071067811865476
INV_SQRT_2PI = 0.3989422804014327
MIB = 2**20
POS_HI = MICRO * GROUP * ROWS
POS_LO = POS_HI + KINDS
POS_GRAD = POS_LO + KINDS


def dot(a, b):
    return lax.dot_general(a, b, (((1,), (0,)), ((), ())), preferred_element_type=F32)


def dot_nt(a, b):
    return lax.dot_general(a, b, (((1,), (1,)), ((), ())), preferred_element_type=F32)


def dot_tn(a, b):
    return lax.dot_general(a, b, (((0,), (0,)), ((), ())), preferred_element_type=F32)


def split(v):
    high = v.astype(BF)
    return high, (v - high.astype(F32)).astype(BF)


def col_sum(v):
    return jnp.sum(v, axis=0, keepdims=True)


def train_kernel(
    lay, inp, cot, slab_in, slab_out, bi, bo, ga, sh, index, table,
    edge, layer_o, input_o, gin_o, gout_o, small_o, gpos_o,
    w_in, w_out, w_in_t, w_out_t, xs, ds, xo, a1, gs, a2, rstd, xf, vec_in, vec, blend, got_in,
    small, small_x, small_sum, small_1, small_2, stat_s, pos_s, layer_s, input_s,
    load_sem, out_load, f_send, f_recv, b_send, b_recv, edge_sem, k_send, k_recv, ready,
    s1_send, s1_recv, s2_send, s2_recv, o_send, o_recv, x_send, x_recv, e_send, i_send, e_recv, own_sem,
    out_sem,
):
    sec = lax.axis_index("section")
    dp = lax.axis_index("dp")
    z, y, c = dp // 8, (dp // 2) % 4, dp % 2
    other = 1 - c
    is_att = sec % 2 == 0
    is_ff = jnp.logical_not(is_att)
    first = sec == 0
    last = sec == 3

    def plus(v, k):
        return lax.rem(v + k, 4)

    def at_dp(zz, yy, cc):
        return {"dp": (zz * 4 + yy) * 2 + cc}

    sibling = at_dp(z, y, other)
    z_peers = {k: at_dp(plus(z, k), y, c) for k in (1, 2, 3)}
    y_peers = {k: at_dp(z, plus(y, k), c) for k in (1, 2, 3)}
    x_peers = {k: {"section": plus(sec, k)} for k in (1, 2, 3)}

    def remote(src, dst, send, recv, device):
        return pltpu.make_async_remote_copy(
            src_ref=src, dst_ref=dst, send_sem=send, recv_sem=recv, device_id=device,
            device_id_type=MESH)

    load_x = pltpu.make_async_copy(inp, xs, load_sem.at[4])
    load_d = pltpu.make_async_copy(cot, ds.at[0], load_sem.at[5])

    def load_out(n):
        return pltpu.make_async_copy(
            slab_out.at[0, pl.ds(pl.multiple_of(n * 128, 128), 128)],
            w_out.at[pl.ds(pl.multiple_of((n % 2) * HALF + (n // 2) * 128, 128), 128)],
            out_load.at[n])

    def load_in(part):
        cols = slice(part * D, (part + 1) * D)
        return pltpu.make_async_copy(slab_in.at[0, :, cols], w_in.at[:, cols], load_sem.at[part])

    @pl.when(first)
    def _():
        load_x.start()

    for part in range(4):
        load_in(part).start()

    @pl.when(is_ff)
    def _():
        def start(n, carry):
            load_out(n).start()
            return carry

        lax.fori_loop(0, 32, start, 0)

    @pl.when(last)
    def _():
        load_d.start()

    barrier = pltpu.get_barrier_semaphore()
    partners = [sibling] + [peers[k] for peers in (x_peers, y_peers, z_peers) for k in (1, 2, 3)]
    for partner in partners:
        pl.semaphore_signal(barrier, inc=1, device_id=partner, device_id_type=MESH)

    vec_in[...] = jnp.zeros_like(vec_in)
    vec[...] = jnp.zeros_like(vec)
    rstd[...] = jnp.zeros_like(rstd)
    gain = ga[...].astype(F32)
    shift = sh[...].astype(F32)
    bias_out = bo[...].astype(F32)

    def forward_copy(m):
        return remote(xo.at[m], xs.at[m], f_send.at[m], f_recv.at[m], x_peers[1])

    def backward_copy(m):
        return remote(xo.at[m], ds.at[0, m], b_send.at[m], b_recv.at[m], x_peers[3])

    def rows_of(m):
        return pl.ds(pl.multiple_of(m * ROWS, ROWS), ROWS)

    def keep_copy(kind, m):
        rows = rows_of(m)
        if kind == "normed":
            n, src, dst = 0, a1.at[0, rows], a1.at[1, rows]
        elif kind == "act":
            n, src, dst = 1, a2.at[2, rows], a2.at[1, rows]
        elif kind == "mixed":
            n, src, dst = 1, a2.at[0, rows, 0:D], a2.at[1, rows, 0:D]
        elif kind == "inner":
            n, src, dst = 2, gs.at[2, rows], gs.at[1, rows]
        else:
            n, src, dst = 3, ds.at[0, m], ds.at[1, m]
        return remote(src, dst, k_send.at[n, m], k_recv.at[n, m], sibling)

    def columns(ref, s):
        return ref.at[:, :, pl.ds(pl.multiple_of(s * 256, 256), 256)]

    def layer_copy(k):
        return remote(columns(xs, plus(sec, k)), layer_s, e_send.at[k - 1], e_recv.at[MICRO],
                      x_peers[k])

    def input_copy(k, m):
        at = pl.ds(pl.multiple_of(plus(sec, k) * 256, 256), 256)
        return remote(xo.at[m, :, at], input_s.at[m], i_send.at[k - 1, m], e_recv.at[m], x_peers[k])

    def own_edge(s, landing):
        return pltpu.make_async_copy(columns(xo if s == 0 else xs, s), landing, own_sem.at[0])

    def edge_save(m):
        return pltpu.make_async_copy(xo.at[m], edge.at[m], edge_sem.at[m])

    def ends_of(m):
        ends, total = [], jnp.int32(0)
        for k in range(SLOTS):
            kind = lay[k, 0, m]
            total = total + jnp.where(kind == 1, SHORT, jnp.where(kind == 2, LONG, 0))
            ends.append(total)
        return ends

    def segment(ends, ids):
        return jnp.where(
            ids < ends[0], 0, jnp.where(ids < ends[1], 1, jnp.where(ids < ends[2], 2, -1)))

    def keep_of(m):
        ends = ends_of(m)
        return (lax.broadcasted_iota(I32, (ROWS, 1), 0) < ends[2]).astype(F32)

    def places(m):
        ends = ends_of(m)
        ids = lax.broadcasted_iota(I32, (ROWS, 1), 0)
        starts = [jnp.int32(0), ends[0], ends[1]]
        place = jnp.full((ROWS, 1), -1, I32)
        for k in range(SLOTS):
            offset = ids - starts[k]
            blended = (lay[k, 0, m] == 2) & (offset >= 1)
            kind = jnp.where(blended, offset - 1, offset + (LONG - 1))
            place = jnp.where((offset >= 0) & (ids < ends[k]), kind, place)
        return (place == lax.broadcasted_iota(I32, (ROWS, KINDS), 1)).astype(F32).astype(BF)

    def build_blend():
        blend[0:8, :] = jnp.full((8, KINDS), -1.0, F32)
        blend[0:CORNERS, 0:LONG - 1] = index[...].astype(F32)
        ids = blend[0:8, :]
        t = lax.broadcasted_iota(I32, (128, KINDS), 0)
        kind = lax.broadcasted_iota(I32, (128, KINDS), 1)
        tf = t.astype(F32)
        total = jnp.where((kind - (LONG - 1) == t) & (t < SHORT), 1.0, 0.0)
        for corner in range(CORNERS):
            weight = (CORNERS - corner) / (CORNERS * (CORNERS + 1) / 2.0)
            total = total + jnp.where(ids[corner:corner + 1, :] == tf, weight, 0.0)
        blend[...] = total

    def norm(m, rows, x):
        mean = jnp.mean(x, axis=1, keepdims=True)
        centered = x - mean
        variance = jnp.mean(centered * centered, axis=1, keepdims=True)
        scale = lax.rsqrt(variance + LN_EPSILON)
        hat = centered * scale
        lane = lax.broadcasted_iota(I32, (ROWS, 128), 1)
        rstd[...] = jnp.where(lane == m, scale, rstd[...])
        xs[m] = hat.astype(BF)
        a1[0, rows, :] = (hat * gain + shift).astype(BF)

    def norm_back(m, rows, d_normed, d):
        hat = xs[m].astype(F32)
        vec[1:2, :] += col_sum(d_normed * hat)
        vec[2:3, :] += col_sum(d_normed)
        e = gain * d_normed
        mean_e = jnp.mean(e, axis=1, keepdims=True)
        mean_eh = jnp.mean(e * hat, axis=1, keepdims=True)
        lane = lax.broadcasted_iota(I32, (ROWS, 128), 1)
        scale = jnp.sum(jnp.where(lane == m, rstd[...], 0.0), axis=1, keepdims=True)
        return d + scale * (e - mean_e - hat * mean_eh)

    def finish_forward(m, branch):
        out = xf[...] + branch
        xo[m] = out.astype(BF)

        @pl.when(sec < 3)
        def _():
            forward_copy(m).start()

        @pl.when(last)
        def _():
            edge_save(m).start()

        keep = keep_of(m)
        vec[3:4, :] += col_sum(keep * out * out)
        vec[4:5, :] += col_sum(keep * branch * branch)

    def finish_backward(m, d_prev):
        @pl.when(sec < 3)
        def _():
            forward_copy(m).wait_send()

        @pl.when(last)
        def _():
            edge_save(m).wait()

        xo[m] = d_prev.astype(BF)

        @pl.when(sec > 0)
        def _():
            backward_copy(m).start()

        @pl.when(first)
        def _():
            for k in (1, 2, 3):
                input_copy(k, m).start()


    def transpose_in():
        def step(i, carry):
            cols = pl.ds(pl.multiple_of(i * 256, 256), 256)
            w_in_t[cols, :] = w_in[:, cols].T
            return carry

        lax.fori_loop(0, FF // 256, step, 0)

    def transpose_out():
        def step(i, carry):
            for core in (0, 1):
                cols = pl.ds(pl.multiple_of(i * 256 + core * 128, 128), 128)
                rows = pl.ds(pl.multiple_of(core * HALF + i * 128, 128), 128)
                w_out_t[:, cols] = w_out[rows, :].T
            return carry

        lax.fori_loop(0, FF // 256, step, 0)

    lane_head = lax.broadcasted_iota(I32, (1, WIDE), 1) // HEAD_DIM
    masks = [(lane_head == h).astype(F32) for h in range(GROUP)]
    masks_low = [m.astype(BF) for m in masks]

    def spread(v):
        return jnp.concatenate([v * mask for mask in masks_low], axis=0)

    def gather_heads(v):
        v = v.reshape(GROUP, ROWS, WIDE)
        return v[0] * masks[0] + v[1] * masks[1] + v[2] * masks[2] + v[3] * masks[3]

    def probs_at(m, g):
        return w_out.at[pl.ds(pl.multiple_of(m * 640, 640), 640), g * WIDE:g * WIDE + ROWS]

    def half_at(part):
        return jnp.where(part // 2 == c, 0, 2), slice((part % 2) * D, (part % 2 + 1) * D)

    def core_slot(core):
        return jnp.where(core == c, 0, 2)

    def attention_forward(m):
        rows = rows_of(m)

        @pl.when(sec > 0)
        def _():
            forward_copy(m).wait_recv()

        xf[...] = xs[m].astype(F32)

        @pl.when(first)
        def _():
            hot = places(m)
            xf[...] += dot(hot, w_out[POS_HI:POS_LO, :]) + dot(hot, w_out[POS_LO:POS_GRAD, :])

        norm(m, rows, xf[...])
        keep_copy("normed", m).start()
        for part in range(3):
            @pl.when(first & (m == 0))
            def _():
                load_in(part).wait()

            cols = slice(part * D, (part + 1) * D)
            proj = dot(a1[0, rows, :], w_in[:, cols])
            if part != 1:
                proj = proj + bi[:, cols].astype(F32)
            slot, at = ((0, D), (2, 0), (2, D))[part]
            a2[slot, rows, at:at + D] = proj.astype(BF)

        @pl.when(first & (m == 0))
        def _():
            load_in(3).wait()

        ends = ends_of(m)
        seg_rows = segment(ends, lax.broadcasted_iota(I32, (ROWS, ROWS), 0))
        seg_cols = segment(ends, lax.broadcasted_iota(I32, (ROWS, ROWS), 1))
        same = seg_rows == seg_cols
        for g in range(D // WIDE):
            lo = D + g * WIDE
            q = spread(a2[0, rows, lo:lo + WIDE])
            k = a2[2, rows, lo - D:lo - D + WIDE]
            v = a2[2, rows, lo:lo + WIDE]
            s = dot_nt(q, k).reshape(GROUP, ROWS, ROWS) * HEAD_DIM ** (-0.5)
            s = jnp.where(same[None], s, MASKED_SCORE)
            s = jnp.exp(s - jnp.max(s, axis=2, keepdims=True))
            p = s * (1.0 / jnp.sum(s, axis=2, keepdims=True))
            p = p.reshape(GROUP * ROWS, ROWS).astype(BF)
            probs_at(m, g)[...] = p
            a2[0, rows, g * WIDE:(g + 1) * WIDE] = gather_heads(dot(p, v)).astype(BF)
        keep_copy("mixed", m).start()
        finish_forward(m, dot(a2[0, rows, 0:D], w_in[:, 3 * D:4 * D]) + bias_out)

    def attention_backward(m):
        rows = rows_of(m)
        backward_copy(m).wait_recv()
        d = ds[0, m]
        slot, cols = half_at(3)
        gs[slot, rows, cols] = d
        vec[0:1, :] += col_sum(d.astype(F32))
        d_mixed = dot(d, w_in_t[3 * D:4 * D, :]).astype(BF)
        for g in range(D // WIDE):
            lo = D + g * WIDE
            q = spread(a2[0, rows, lo:lo + WIDE])
            k = a2[2, rows, lo - D:lo - D + WIDE]
            v = a2[2, rows, lo:lo + WIDE]
            dm = spread(d_mixed[:, g * WIDE:(g + 1) * WIDE])
            p = probs_at(m, g)[...]
            dp_ = dot_nt(dm, v)
            pf = p.astype(F32)
            row_dot = jnp.sum(pf * dp_, axis=1, keepdims=True)
            d_s = (pf * (dp_ - row_dot)).astype(BF)
            dq = (gather_heads(dot(d_s, k)) * HEAD_DIM ** (-0.5)).astype(BF)
            dk = (dot_tn(d_s, q) * HEAD_DIM ** (-0.5)).astype(BF)
            dv = dot_tn(p, dm).astype(BF)
            low = slice(g * WIDE, (g + 1) * WIDE)
            high = slice(D + g * WIDE, D + (g + 1) * WIDE)
            gs[half_at(0)[0], rows, low] = dq
            gs[half_at(1)[0], rows, high] = dk
            gs[half_at(2)[0], rows, low] = dv
            vec_in[0:1, low] += col_sum(dq.astype(F32))
            vs = slice(2 * D + g * WIDE, 2 * D + (g + 1) * WIDE)
            vec_in[0:1, vs] += col_sum(dv.astype(F32))
        keep_copy("inner", m).start()
        d_normed = dot(gs[half_at(0)[0], rows, :], w_in_t[0:2 * D, :])
        d_normed = d_normed + dot(gs[half_at(2)[0], rows, 0:D], w_in_t[2 * D:3 * D, :])
        finish_backward(m, norm_back(m, rows, d_normed, d.astype(F32)))

        @pl.when(first)
        def _():
            at = pl.ds(pl.multiple_of(POS_GRAD + m * KINDS, KINDS), KINDS)
            w_out[at, :] = dot_tn(places(m), xo[m]).astype(BF)

    def feed_forward(m):
        rows = rows_of(m)
        forward_copy(m).wait_recv()
        xf[...] = xs[m].astype(F32)
        norm(m, rows, xf[...])
        keep_copy("normed", m).start()
        for part in range(4):
            cols = slice(part * D, (part + 1) * D)
            v = dot(a1[0, rows, :], w_in[:, cols]) + bi[:, cols].astype(F32)
            cdf = 0.5 + 0.5 * lax.erf(v * INV_SQRT2)
            act = (v * cdf).astype(BF)
            for n in range(8):
                chip, core = part * 4 + n // 2, n % 2
                a2[core_slot(core), rows, chip * 128:(chip + 1) * 128] = act[:, n * 128:(n + 1) * 128]
            slot, at = half_at(part)
            gs[slot, rows, at] = (cdf + v * (INV_SQRT_2PI * jnp.exp(-0.5 * v * v))).astype(BF)
        keep_copy("act", m).start()
        branch = dot(a2[core_slot(0), rows, :], w_out[0:HALF, :])
        branch = branch + dot(a2[core_slot(1), rows, :], w_out[HALF:FF, :])
        finish_forward(m, branch + bias_out)

    def feed_backward(m):
        rows = rows_of(m)

        @pl.when(sec < 3)
        def _():
            backward_copy(m).wait_recv()

        @pl.when(last)
        def _():
            ds[0, m] = (ds[0, m].astype(F32) * keep_of(m)).astype(BF)

        keep_copy("branch", m).start()
        d = ds[0, m]
        vec[0:1, :] += col_sum(d.astype(F32))
        for part in range(4):
            cols = slice(part * D, (part + 1) * D)
            slot, at = half_at(part)
            d_act = dot(d, w_out_t[:, cols])
            d_inner = (d_act * gs[slot, rows, at].astype(F32)).astype(BF)
            gs[slot, rows, at] = d_inner
            vec_in[0:1, cols] += col_sum(d_inner.astype(F32))
        keep_copy("inner", m).start()
        d_normed = dot(gs[half_at(0)[0], rows, :], w_in_t[0:HALF, :])
        d_normed = d_normed + dot(gs[half_at(2)[0], rows, :], w_in_t[HALF:FF, :])
        finish_backward(m, norm_back(m, rows, d_normed, d.astype(F32)))

    def say_ready():
        for peer in (z_peers[1], z_peers[3], y_peers[1], y_peers[3]):
            pl.semaphore_signal(ready, inc=1, device_id=peer, device_id_type=MESH)


    coords = ((z, y), (y, z), (z, y))
    peers = ((z_peers, y_peers), (y_peers, z_peers), (z_peers, y_peers))
    sets = (0, 1, 2)

    def start_small(height):
        def cross():
            return remote(small.at[:, :, other, 0:height], small_x.at[:, :, 0:height], o_send.at[2],
                          o_recv.at[2], sibling)

        count = jnp.int32(0)
        for k in (1, 2, 3):
            stat_copy(k).wait_recv()
        for j in range(32):
            quad = slice((j // 4) * 128, (j // 4 + 1) * 128)
            at = (j // 8, (j // 2) % 4, j % 2)
            small[at + (slice(0, 1),)] = vec_in[0:1, j * 128:(j + 1) * 128]
            small[at + (slice(1, 4),)] = vec[0:3, quad]
            for s in range(4):
                small[at + (slice(4 + s, 5 + s),)] = stat_s[s, 0:1, :]
        cross().start()
        return cross

    def reduce(block_of, land1_of, land2_of, half, height, make, between):
        def block(s, a, b):
            return small_sum.at[a, b, 0:height] if s == 2 else block_of(s, a, b)

        def land1(s, i, q):
            return small_1.at[i, q, 0:height] if s == 2 else land1_of(s, i, q)

        def land2(s, i):
            return small_2.at[i, 0:height // 2] if s == 2 else land2_of(s, i)

        def target(p, i):
            return {0: (plus(p, 2), 0), 1: (plus(p, 2), 1), 2: (plus(p, 1), 1),
                    3: (plus(p, 3), 0), 4: (plus(p, 1), 0), 5: (plus(p, 3), 1)}[i]

        def step1(s, i, q):
            a, h = target(coords[s][0], i)
            peer = peers[s][0][1 if i % 2 == 0 else 3]
            return remote(block(s, a, 2 * h + q), land1(s, i, q), s1_send.at[s, i, q],
                          s1_recv.at[s, i, q], peer)

        def half_of(s, b, h):
            return block(s, coords[s][0], b).at[h * half[s]:(h + 1) * half[s], :]

        def step2(s, i):
            b, h = target(coords[s][1], i)
            peer = peers[s][1][1 if i % 2 == 0 else 3]
            return remote(half_of(s, b, h), land2(s, i), s2_send.at[s, i], s2_recv.at[s, i], peer)

        def add(ref, *others):
            total = ref[...].astype(F32)
            for o in others:
                total = total + o[...].astype(F32)
            ref[...] = total.astype(ref.dtype)

        cross = start_small(height)
        for n, pieces in ((2, (0, 1)), (1, (2,)), (3, (3,)), (0, ())):
            for s in (0, 1):
                make(s, plus(coords[s][0], n), n)
                if s == 0 and n == 2:
                    pl.semaphore_wait(ready, 4)
                    cross().wait_recv()
                    small_sum[:, :, 0:height] = small[:, :, c, 0:height] + small_x[:, :, 0:height]
                    for i in (0, 1, 2, 3):
                        for q in (0, 1):
                            step1(2, i, q).start()
                for i in pieces:
                    for q in (0, 1):
                        step1(s, i, q).start()
        for i in (4, 5):
            for q in (0, 1):
                for s in (2, 0, 1):
                    a, h = target(coords[s][0], i)
                    step1(s, i - 4, q).wait_recv()
                    add(block(s, a, 2 * h + q), land1(s, i - 4, q))
                    step1(s, i, q).start()
        between()
        for s in sets:
            for i in (2, 3, 4, 5):
                for q in (0, 1):
                    step1(s, i, q).wait_recv()
        for n, pieces in ((2, (0, 1)), (1, (2,)), (3, (3,)), (0, ())):
            for s in sets:
                p1, p2 = coords[s]
                b = plus(p2, n)
                h, q = b // 2, b % 2
                add(block(s, p1, b), land1(s, jnp.where(h == 0, 4, 2), q),
                    land1(s, jnp.where(h == 0, 3, 5), q))
                for i in pieces:
                    step2(s, i).start()
        for i in (4, 5):
            for s in sets:
                b, h = target(coords[s][1], i)
                step2(s, i - 4).wait_recv()
                add(half_of(s, b, h), land2(s, i - 4))
                step2(s, i).start()
        for s in sets:
            p2 = coords[s][1]
            for h, up, down in ((0, 4, 3), (1, 2, 5)):
                step2(s, up).wait_recv()
                step2(s, down).wait_recv()
                add(half_of(s, p2, h), land2(s, up), land2(s, down))
        small_o[...] = small_sum[z, y, 0:8]

        def finish():
            cross().wait_send()
            for s in sets:
                for i in range(6):
                    for q in (0, 1):
                        step1(s, i, q).wait_send()
                    step2(s, i).wait_send()

        return finish

    def stat_copy(k):
        return remote(stat_s.at[sec], stat_s.at[sec], x_send.at[k - 1], x_recv.at[k - 1],
                      x_peers[k])

    def send_stats():
        count = jnp.int32(0)
        for m in range(MICRO):
            count = count + ends_of(m)[2]
        lanes = lax.broadcasted_iota(I32, (8, 128), 1)
        stream_sq = jnp.sum(vec[3:4, :], axis=1, keepdims=True)
        branch_sq = jnp.sum(vec[4:5, :], axis=1, keepdims=True)
        stat_s[sec] = jnp.where(
            lanes == 0, stream_sq,
            jnp.where(lanes == 1, branch_sq, jnp.where(lanes == 2, count.astype(F32), 0.0)))
        for k in (1, 2, 3):
            stat_copy(k).start()

    def both(ref, start, width, *cols):
        return ref[:, :, pl.ds(pl.multiple_of(start, width), width)].reshape(2 * ALL, width).T

    def kept(n):
        for m in range(MICRO):
            keep_copy(n, m).wait_recv()

    def kept_sent(n):
        for m in range(MICRO):
            keep_copy(n, m).wait_send()

    def pos_copy(k):
        return remote(pos_s, pos_s, x_send.at[2 + k], x_recv.at[3], x_peers[k])

    def own_copy(n, src, dst):
        return remote(src, dst, o_send.at[n], o_recv.at[n], sibling)

    @pl.when(first)
    def _():
        build_blend()
        high, low = split(blend[0:SHORT, :])
        rows = dot_tn(high, table[...]) + dot_tn(low, table[...])
        w_out[POS_HI:POS_LO, :], w_out[POS_LO:POS_GRAD, :] = split(rows)
        load_x.wait()

    pl.semaphore_wait(barrier, len(partners))

    @pl.when(is_att)
    def _():
        @pl.when(sec > 0)
        def _():
            for part in range(4):
                load_in(part).wait()
            transpose_in()

        def fwd(m, carry):
            attention_forward(m)
            return carry

        lax.fori_loop(0, MICRO, fwd, 0)

        @pl.when(first)
        def _():
            transpose_in()

        send_stats()
        say_ready()

        def bwd(m, carry):
            attention_backward(m)
            return carry

        lax.fori_loop(0, MICRO, bwd, 0)

        @pl.when(first)
        def _():
            own_edge(0, input_s).start()

        kept("normed")
        kept("mixed")
        kept("inner")

        def block(s, a, b):
            zz, yy = (a, b) if s == 0 else (b, a)
            at = pl.ds(pl.multiple_of(zz * 256 + yy * 64, 64), 64)
            return w_out_t.at[at, s * D:(s + 1) * D]

        def land1(s, i, q):
            at = pl.ds(pl.multiple_of((i * 2 + q) * 64, 64), 64)
            return w_in.at[at, s * HALF:s * HALF + D]

        def land2(s, i):
            return w_in.at[768 + i * 32:768 + (i + 1) * 32, s * HALF:s * HALF + D]

        def make(s, a, n):
            if s == 1:
                if n == 2:
                    make_second()
            else:
                at = pl.ds(pl.multiple_of(a * 256, 256), 256)
                lhs = both(a1, a * 256, 256)
                rhs = gs[0:2, :, 0:D].reshape(2 * ALL, D)
                w_out_t[at, 0:D] = dot(lhs, rhs).astype(BF)

        def make_second():
            def step(zz, carry):
                at = pl.ds(pl.multiple_of(zz * 256, 256), 256)
                lhs = jnp.where(c == 0, both(a1, zz * 256, 256), both(a2.at[0:2], zz * 256, 256))
                rhs = gs[0:2, :, D:2 * D].reshape(2 * ALL, D)
                w_out_t[at, D:2 * D] = dot(lhs, rhs).astype(BF)
                return carry

            lax.fori_loop(0, 4, step, 0)

        small[...] = jnp.zeros_like(small)

        @pl.when(first)
        def _():
            total = jnp.zeros((128, D), F32)
            grads = w_out[POS_GRAD:POS_GRAD + MICRO * KINDS, :].reshape(MICRO, KINDS, D)
            b_hi, b_lo = split(blend[...])
            for m in range(MICRO):
                total = total + dot(b_hi, grads[m]) + dot(b_lo, grads[m])
            for pair in (0, 1):
                both_sections = jnp.concatenate(
                    [total[0:64, (2 * pair + n) * 256:(2 * pair + n + 1) * 256] for n in (0, 1)],
                    axis=0)
                at = slice(8 + pair * 8, 16 + pair * 8)
                small[:, :, :, at] = both_sections.T.reshape(4, 4, 2, 8, 128)

        finish = reduce(block, land1, land2, (32, 32, 16), 32, make, lambda: None)

        def sent(n):
            return block(n, coords[n][0], coords[n][1]).at[
                pl.ds(pl.multiple_of(other * 32, 32), 32), :]

        def mine(n):
            return block(n, coords[n][0], coords[n][1]).at[
                pl.ds(pl.multiple_of(c * 32, 32), 32), :]

        def swap(n):
            return own_copy(n, sent(n), got_in.at[:, n * D:(n + 1) * D])

        for n in (0, 1):
            swap(n).start()

        @pl.when(first)
        def _():
            pos_s[...] = small_sum[z, y, 8:24]
            for k in (1, 2, 3):
                pos_copy(k).start()

        for n in (0, 1):
            swap(n).wait_recv()
        copies = [
            pltpu.make_async_copy(mine(n), gin_o.at[c, :, n * D:(n + 1) * D], out_sem.at[n])
            for n in (0, 1)]
        copies.append(pltpu.make_async_copy(got_in, gin_o.at[other], out_sem.at[2]))
        for copy in copies:
            copy.start()
        finish()
        for n in (0, 1):
            swap(n).wait_send()
        for copy in copies:
            copy.wait()
        kept_sent("normed")
        kept_sent("mixed")
        kept_sent("inner")

    @pl.when(is_ff)
    def _():
        for part in range(4):
            load_in(part).wait()

        def arrived(n, carry):
            load_out(n).wait()
            return carry

        lax.fori_loop(0, 32, arrived, 0)

        @pl.when(last)
        def _():
            load_d.wait()

        def tick(t, carry):
            @pl.when((last & (t == 0)) | (jnp.logical_not(last) & (t == MICRO)))
            def _():
                transpose_out()
                transpose_in()

            @pl.when((last & (t == 2 * MICRO - 1)) | (jnp.logical_not(last) & (t == MICRO)))
            def _():
                say_ready()

            @pl.when(jnp.logical_not(last) & (t == MICRO))
            def _():
                send_stats()

            is_fwd = (last & (t % 2 == 0)) | (jnp.logical_not(last) & (t < MICRO))
            m = jnp.where(last, t // 2, t % MICRO)

            @pl.when(is_fwd)
            def _():
                feed_forward(m)

            @pl.when(jnp.logical_not(is_fwd))
            def _():
                feed_backward(m)

            return carry

        lax.fori_loop(0, 2 * MICRO, tick, 0)

        @pl.when(last)
        def _():
            send_stats()
            pltpu.make_async_copy(edge, xs, load_sem.at[4]).start()

        for n in ("normed", "act", "branch", "inner"):
            kept(n)

        def block(s, a, b):
            if s == 0:
                at = pl.ds(pl.multiple_of(a * 256 + b * 64, 64), 64)
                return w_out_t.at[at, 0:HALF]
            at = pl.ds(pl.multiple_of(b * 512 + a * 128, 128), 128)
            return w_in_t.at[at, :]

        def land1(s, i, q):
            n = i * 2 + q
            if s == 0:
                return w_in.at[pl.ds(pl.multiple_of(n * 64, 64), 64), 0:HALF]
            rows = pl.ds(pl.multiple_of((n % 8) * 128, 128), 128)
            return w_in.at[rows, pl.ds(pl.multiple_of(HALF + (n // 8) * D, D), D)]

        def land2(s, i):
            if s == 0:
                return w_in.at[768 + i * 32:768 + (i + 1) * 32, 0:HALF]
            return w_in.at[512 + i * 64:512 + (i + 1) * 64, FF - D:FF]

        def make(s, a, n):
            if s == 0:
                at = pl.ds(pl.multiple_of(a * 256, 256), 256)
                lhs = both(a1, a * 256, 256)
                for n in (0, 1):
                    cols = slice(n * D, (n + 1) * D)
                    rhs = gs[0:2, :, cols].reshape(2 * ALL, D)
                    w_out_t[at, cols] = dot(lhs, rhs).astype(BF)
            else:
                def step(pair, carry):
                    lhs = []
                    for n in (0, 1):
                        chip = (pair * 2 + n) * 4 + a
                        lhs.append(both(a2.at[0:2], chip * 128, 128))
                    rhs = ds[...].reshape(2 * ALL, D)
                    block2 = dot(jnp.concatenate(lhs, axis=0), rhs).astype(BF)
                    for n in (0, 1):
                        chip = (pair * 2 + n) * 4 + a
                        at = pl.ds(pl.multiple_of(chip * 128, 128), 128)
                        w_in_t[at, :] = block2[n * 128:(n + 1) * 128, :]
                    return carry

                lax.fori_loop(0, 2, step, 0)

        small[...] = jnp.zeros_like(small)
        def between():
            @pl.when(last)
            def _():
                pltpu.make_async_copy(edge, xs, load_sem.at[4]).wait()
                for k in (1, 2, 3):
                    layer_copy(k).start()
                own_edge(3, layer_s).start()

        finish = reduce(block, land1, land2, (32, 64, 8), 16, make, between)

        def part(core):
            return block(0, z, y).at[pl.ds(pl.multiple_of(core * 32, 32), 32), :]

        swap = own_copy(0, part(other), got_in)
        swap.start()
        swap.wait_recv()
        copies = [
            pltpu.make_async_copy(src, dst, out_sem.at[n]) for n, (src, dst) in enumerate((
                (part(c), gin_o.at[c]), (got_in, gin_o.at[other]), (block(1, y, z), gout_o)))]
        for copy in copies:
            copy.start()
        finish()
        swap.wait_send()
        for copy in copies:
            copy.wait()
        for n in ("normed", "act", "branch", "inner"):
            kept_sent(n)

    @pl.when(first)
    def _():
        own_edge(0, input_s).wait()
        layer_copy(1).wait_recv()

    @pl.when(sec > 0)
    def _():
        for m in range(MICRO):
            input_copy(1, m).wait_recv()

        @pl.when(sec < 3)
        def _():
            layer_copy(1).wait_recv()

        @pl.when(last)
        def _():
            own_edge(3, layer_s).wait()

    outs = [pltpu.make_async_copy(layer_s, layer_o, out_sem.at[3]),
            pltpu.make_async_copy(input_s, input_o, out_sem.at[4])]
    for copy in outs:
        copy.start()

    @pl.when(sec > 0)
    def _():
        pos_copy(1).wait_recv()

        for m in range(MICRO):
            backward_copy(m).wait_send()

    gpos_o[...] = pos_s[...]
    for k in (1, 2, 3):
        stat_copy(k).wait_send()

    @pl.when(first)
    def _():
        for k in (1, 2, 3):
            pos_copy(k).wait_send()
            for m in range(MICRO):
                input_copy(k, m).wait_send()

    @pl.when(last)
    def _():
        for k in (1, 2, 3):
            layer_copy(k).wait_send()

    for copy in outs:
        copy.wait()


def output_kernel(
    layer, inp, gin, gout, small, gpos,
    layer_o, input_o, gin_o, gout_o, bin_o, bout_o, gain_o, shift_o, pos_o, stats_o,
):
    sec = lax.axis_index("section")
    quarter = lax.axis_index("dp") % 4
    layer_o[...] = layer[...]
    input_o[...] = inp[...]
    for half in (0, 1):
        gin_o[0, :, half * HALF:(half + 1) * HALF] = gin[half].astype(F32)

    @pl.when(sec % 2 == 0)
    def _():
        gout_o[...] = jnp.zeros_like(gout_o)

    @pl.when(sec % 2 == 1)
    def _():
        gout_o[0] = gout[...].astype(F32)

    bin_o[...] = small[0:1, :]
    for row, ref in ((1, bout_o), (2, gain_o), (3, shift_o)):
        line = small[row:row + 1, :]
        picked = line[:, 0:32]
        for n in (1, 2, 3):
            picked = jnp.where(quarter == n, line[:, n * 32:(n + 1) * 32], picked)
        ref[...] = picked
    pair = jnp.where(sec < 2, gpos[0:8, :], gpos[8:16, :])
    pos_o[...] = jnp.where(sec % 2 == 0, pair[:, 0:SHORT], pair[:, 64:64 + SHORT])
    count = small[4:5, 2:3]
    kind = lax.broadcasted_iota(I32, (2, 4), 0)
    section = lax.broadcasted_iota(I32, (2, 4), 1)
    total = jnp.zeros((2, 4), F32)
    for s in range(4):
        for r in range(2):
            total = jnp.where(
                (kind == r) & (section == s), small[4 + s:5 + s, r:r + 1], total)
    stats_o[...] = jnp.sqrt(total / (count * D))


def local(inputs, cotangent, layout, pos_index, pos_table, slab_in, slab_out, bias_in, bias_out,
          ln_gain, ln_bias):
    shape = jax.ShapeDtypeStruct
    vmem = pl.BlockSpec(memory_space=pltpu.VMEM)
    smem = pl.BlockSpec(memory_space=pltpu.SMEM)
    anywhere = pl.BlockSpec(memory_space=pl.ANY)
    dma = pltpu.SemaphoreType.DMA

    edge, *parts = pl.pallas_call(
        train_kernel,
        name="train",
        out_shape=(
            shape((MICRO, ROWS, D), BF), shape((MICRO, ROWS, 256), BF),
            shape((MICRO, ROWS, 256), BF), shape((2, 32, HALF), BF), shape((128, D), BF),
            shape((8, 128), F32), shape((16, 128), F32)),
        in_specs=[smem] + [anywhere] * 4 + [vmem] * 6,
        out_specs=(anywhere,) * 5 + (vmem,) * 2,
        scratch_shapes=[
            pltpu.VMEM((D, FF), BF), pltpu.VMEM((FF, D), BF),
            pltpu.VMEM((FF, D), BF), pltpu.VMEM((D, FF), BF),
            pltpu.VMEM((MICRO, ROWS, D), BF), pltpu.VMEM((2, MICRO, ROWS, D), BF),
            pltpu.VMEM((MICRO, ROWS, D), BF),
            pltpu.VMEM((2, ALL, D), BF), pltpu.VMEM((3, ALL, HALF), BF),
            pltpu.VMEM((3, ALL, HALF), BF),
            pltpu.VMEM((ROWS, 128), F32), pltpu.VMEM((ROWS, D), F32),
            pltpu.VMEM((8, FF), F32), pltpu.VMEM((8, D), F32), pltpu.VMEM((128, KINDS), F32),
            pltpu.VMEM((32, HALF), BF),
            pltpu.VMEM((4, 4, 2, 32, 128), F32), pltpu.VMEM((4, 4, 32, 128), F32),
            pltpu.VMEM((4, 4, 32, 128), F32), pltpu.VMEM((6, 2, 32, 128), F32),
            pltpu.VMEM((6, 16, 128), F32), pltpu.VMEM((4, 8, 128), F32),
            pltpu.VMEM((16, 128), F32),
            pltpu.VMEM((MICRO, ROWS, 256), BF), pltpu.VMEM((MICRO, ROWS, 256), BF),
            dma((6,)), dma((32,)), dma((MICRO,)), dma((MICRO,)), dma((MICRO,)), dma((MICRO,)),
            dma((MICRO,)), dma((4, MICRO)), dma((4, MICRO)), pltpu.SemaphoreType.REGULAR,
            dma((3, 6, 2)), dma((3, 6, 2)), dma((3, 6)), dma((3, 6)), dma((3,)), dma((3,)),
            dma((6,)), dma((4,)), dma((3,)), dma((3, MICRO)), dma((MICRO + 1,)), dma((1,)), dma((5,)),
        ],
        compiler_params=pltpu.CompilerParams(
            collective_id=0, has_side_effects=True, vmem_limit_bytes=62 * MIB),
    )(layout.transpose(2, 1, 0), inputs, cotangent, slab_in, slab_out, bias_in, bias_out, ln_gain,
      ln_bias, pos_index.T, pos_table)

    *grads, grad_pos, stats = pl.pallas_call(
        output_kernel,
        name="outputs",
        out_shape=(
            shape((MICRO, ROWS, 256), BF), shape((MICRO, ROWS, 256), BF), shape((1, 32, FF), F32),
            shape((1, 128, D), F32), shape((1, 128), F32), shape((1, 32), F32),
            shape((1, 32), F32), shape((1, 32), F32), shape((8, SHORT), F32), shape((2, 4), F32)),
        in_specs=[vmem] * 6,
        out_specs=(vmem,) * 10,
        compiler_params=pltpu.CompilerParams(vmem_limit_bytes=60 * MIB),
    )(*parts)
    return (*grads, grad_pos.T, stats)


def solution(mesh):
    return jax.shard_map(
        local,
        mesh=mesh,
        in_specs=(
            P(None, "dp", None), P(None, "dp", None), P(None, "dp", None), P(), P(),
            P("section", None, None), P("section", None, None), P("section", None),
            P("section", None), P("section", None), P("section", None)),
        out_specs=(
            P(None, "dp", "section"), P(None, "dp", "section"), P("section", "dp", None),
            P("section", "dp", None), P("section", "dp"), P("section", "dp"),
            P("section", "dp"), P("section", "dp"), P(None, ("section", "dp")), P()),
        check_vma=False,
    )
```

```python
import jax
import jax.numpy as jnp
from jax import lax
from jax.experimental import pallas as pl
from jax.experimental.pallas import tpu as pltpu
from jax.sharding import PartitionSpec as P

BF = jnp.bfloat16
F32 = jnp.float32
I32 = jnp.int32
MESH = pl.DeviceIdType.MESH

D = 1024
FF = 4096
HALF = FF // 2
HEAD_DIM = 64
SHORT = 50
LONG = 145
MICRO = 4
ROWS = 160
ALL = MICRO * ROWS
SLOTS = 3
GROUP = 4
WIDE = GROUP * HEAD_DIM
KINDS = 256
CORNERS = 4
LN_EPSILON = 1e-06
MASKED_SCORE = -1e30
INV_SQRT2 = 0.7071067811865476
INV_SQRT_2PI = 0.3989422804014327
MIB = 2**20
POS_HI = MICRO * GROUP * ROWS
POS_LO = POS_HI + KINDS
POS_GRAD = POS_LO + KINDS


def dot(a, b):
    return lax.dot_general(a, b, (((1,), (0,)), ((), ())), preferred_element_type=F32)


def dot_nt(a, b):
    return lax.dot_general(a, b, (((1,), (1,)), ((), ())), preferred_element_type=F32)


def dot_tn(a, b):
    return lax.dot_general(a, b, (((0,), (0,)), ((), ())), preferred_element_type=F32)


def split(v):
    high = v.astype(BF)
    return high, (v - high.astype(F32)).astype(BF)


def col_sum(v):
    return jnp.sum(v, axis=0, keepdims=True)


def train_kernel(
    lay, inp, cot, slab_in, slab_out, bi, bo, ga, sh, index, table,
    layer_o, input_o, gin_o, gout_o, small_o, gpos_o,
    w_in, w_out, w_in_t, w_out_t, xs, ds, xo, a1, gs, a2, rstd, xf, vec_in, vec, blend, got_in,
    small, small_x, small_sum, small_1, small_2, stat_s, pos_s, layer_s, input_s,
    load_sem, out_load, f_send, f_recv, b_send, b_recv, k_send, k_recv, ready,
    s1_send, s1_recv, s2_send, s2_recv, o_send, o_recv, x_send, x_recv, e_send, i_send, e_recv, own_sem,
    out_sem,
):
    sec = lax.axis_index("section")
    dp = lax.axis_index("dp")
    z, y, c = dp // 8, (dp // 2) % 4, dp % 2
    other = 1 - c
    is_att = sec % 2 == 0
    is_ff = jnp.logical_not(is_att)
    first = sec == 0
    last = sec == 3

    def plus(v, k):
        return lax.rem(v + k, 4)

    def at_dp(zz, yy, cc):
        return {"dp": (zz * 4 + yy) * 2 + cc}

    sibling = at_dp(z, y, other)
    z_peers = {k: at_dp(plus(z, k), y, c) for k in (1, 2, 3)}
    y_peers = {k: at_dp(z, plus(y, k), c) for k in (1, 2, 3)}
    x_peers = {k: {"section": plus(sec, k)} for k in (1, 2, 3)}

    def remote(src, dst, send, recv, device):
        return pltpu.make_async_remote_copy(
            src_ref=src, dst_ref=dst, send_sem=send, recv_sem=recv, device_id=device,
            device_id_type=MESH)

    load_x = pltpu.make_async_copy(inp, xs, load_sem.at[4])
    load_d = pltpu.make_async_copy(cot, ds.at[0], load_sem.at[5])

    def load_out(n):
        return pltpu.make_async_copy(
            slab_out.at[0, pl.ds(pl.multiple_of(n * 128, 128), 128)],
            w_out.at[pl.ds(pl.multiple_of((n % 2) * HALF + (n // 2) * 128, 128), 128)],
            out_load.at[n])

    def load_in(part):
        cols = slice(part * D, (part + 1) * D)
        return pltpu.make_async_copy(slab_in.at[0, :, cols], w_in.at[:, cols], load_sem.at[part])

    @pl.when(first)
    def _():
        load_x.start()

    for part in range(4):
        load_in(part).start()

    @pl.when(is_ff)
    def _():
        def start(n, carry):
            load_out(n).start()
            return carry

        lax.fori_loop(0, 32, start, 0)

    @pl.when(last)
    def _():
        load_d.start()

    barrier = pltpu.get_barrier_semaphore()
    partners = [sibling] + [peers[k] for peers in (x_peers, y_peers, z_peers) for k in (1, 2, 3)]
    for partner in partners:
        pl.semaphore_signal(barrier, inc=1, device_id=partner, device_id_type=MESH)

    vec_in[...] = jnp.zeros_like(vec_in)
    vec[...] = jnp.zeros_like(vec)
    rstd[...] = jnp.zeros_like(rstd)
    gain = ga[...].astype(F32)
    shift = sh[...].astype(F32)
    bias_out = bo[...].astype(F32)

    def forward_copy(m):
        return remote(xo.at[m], xs.at[m], f_send.at[m], f_recv.at[m], x_peers[1])

    def backward_copy(m):
        return remote(xo.at[m], ds.at[0, m], b_send.at[m], b_recv.at[m], x_peers[3])

    def rows_of(m):
        return pl.ds(pl.multiple_of(m * ROWS, ROWS), ROWS)

    def keep_copy(kind, m):
        rows = rows_of(m)
        if kind == "normed":
            n, src, dst = 0, a1.at[0, rows], a1.at[1, rows]
        elif kind == "act":
            n, src, dst = 1, a2.at[2, rows], a2.at[1, rows]
        elif kind == "mixed":
            n, src, dst = 1, a2.at[0, rows, 0:D], a2.at[1, rows, 0:D]
        elif kind == "inner":
            n, src, dst = 2, gs.at[2, rows], gs.at[1, rows]
        else:
            n, src, dst = 3, ds.at[0, m], ds.at[1, m]
        return remote(src, dst, k_send.at[n, m], k_recv.at[n, m], sibling)

    def columns(ref, s):
        return ref.at[:, :, pl.ds(pl.multiple_of(s * 256, 256), 256)]

    def layer_copy(k):
        return remote(columns(xs, plus(sec, k)), layer_s, e_send.at[k - 1], e_recv.at[MICRO],
                      x_peers[k])

    def input_copy(k, m):
        at = pl.ds(pl.multiple_of(plus(sec, k) * 256, 256), 256)
        return remote(xo.at[m, :, at], input_s.at[m], i_send.at[k - 1, m], e_recv.at[m], x_peers[k])

    def own_edge(s, landing):
        return pltpu.make_async_copy(columns(xo if s == 0 else xs, s), landing, own_sem.at[0])

    def ends_of(m):
        ends, total = [], jnp.int32(0)
        for k in range(SLOTS):
            kind = lay[k, 0, m]
            total = total + jnp.where(kind == 1, SHORT, jnp.where(kind == 2, LONG, 0))
            ends.append(total)
        return ends

    def segment(ends, ids):
        return jnp.where(
            ids < ends[0], 0, jnp.where(ids < ends[1], 1, jnp.where(ids < ends[2], 2, -1)))

    def keep_of(m):
        ends = ends_of(m)
        return (lax.broadcasted_iota(I32, (ROWS, 1), 0) < ends[2]).astype(F32)

    def places(m):
        ends = ends_of(m)
        ids = lax.broadcasted_iota(I32, (ROWS, 1), 0)
        starts = [jnp.int32(0), ends[0], ends[1]]
        place = jnp.full((ROWS, 1), -1, I32)
        for k in range(SLOTS):
            offset = ids - starts[k]
            blended = (lay[k, 0, m] == 2) & (offset >= 1)
            kind = jnp.where(blended, offset - 1, offset + (LONG - 1))
            place = jnp.where((offset >= 0) & (ids < ends[k]), kind, place)
        return (place == lax.broadcasted_iota(I32, (ROWS, KINDS), 1)).astype(F32).astype(BF)

    def build_blend():
        blend[0:8, :] = jnp.full((8, KINDS), -1.0, F32)
        blend[0:CORNERS, 0:LONG - 1] = index[...].astype(F32)
        ids = blend[0:8, :]
        t = lax.broadcasted_iota(I32, (128, KINDS), 0)
        kind = lax.broadcasted_iota(I32, (128, KINDS), 1)
        tf = t.astype(F32)
        total = jnp.where((kind - (LONG - 1) == t) & (t < SHORT), 1.0, 0.0)
        for corner in range(CORNERS):
            weight = (CORNERS - corner) / (CORNERS * (CORNERS + 1) / 2.0)
            total = total + jnp.where(ids[corner:corner + 1, :] == tf, weight, 0.0)
        blend[...] = total

    def norm(m, rows, x):
        mean = jnp.mean(x, axis=1, keepdims=True)
        centered = x - mean
        variance = jnp.mean(centered * centered, axis=1, keepdims=True)
        scale = lax.rsqrt(variance + LN_EPSILON)
        hat = centered * scale
        lane = lax.broadcasted_iota(I32, (ROWS, 128), 1)
        rstd[...] = jnp.where(lane == m, scale, rstd[...])
        xs[m] = hat.astype(BF)
        a1[0, rows, :] = (hat * gain + shift).astype(BF)

    def norm_back(m, rows, d_normed, d):
        hat = xs[m].astype(F32)
        vec[1:2, :] += col_sum(d_normed * hat)
        vec[2:3, :] += col_sum(d_normed)
        e = gain * d_normed
        mean_e = jnp.mean(e, axis=1, keepdims=True)
        mean_eh = jnp.mean(e * hat, axis=1, keepdims=True)
        lane = lax.broadcasted_iota(I32, (ROWS, 128), 1)
        scale = jnp.sum(jnp.where(lane == m, rstd[...], 0.0), axis=1, keepdims=True)
        return d + scale * (e - mean_e - hat * mean_eh)

    def add_stats(m, out, branch):
        keep = keep_of(m)
        vec[3:4, :] += col_sum(keep * out * out)
        vec[4:5, :] += col_sum(keep * branch * branch)

    def finish_forward(m, branch):
        out = xf[...] + branch
        xo[m] = out.astype(BF)
        forward_copy(m).start()
        add_stats(m, out, branch)

    def finish_backward(m, d_prev):
        @pl.when(sec < 3)
        def _():
            forward_copy(m).wait_send()

        xo[m] = d_prev.astype(BF)

        @pl.when(sec > 0)
        def _():
            backward_copy(m).start()

        @pl.when(first)
        def _():
            for k in (1, 2, 3):
                input_copy(k, m).start()

    def transpose_in():
        def step(i, carry):
            cols = pl.ds(pl.multiple_of(i * 256, 256), 256)
            w_in_t[cols, :] = w_in[:, cols].T
            return carry

        lax.fori_loop(0, FF // 256, step, 0)

    def transpose_out():
        def step(i, carry):
            for core in (0, 1):
                cols = pl.ds(pl.multiple_of(i * 256 + core * 128, 128), 128)
                rows = pl.ds(pl.multiple_of(core * HALF + i * 128, 128), 128)
                w_out_t[:, cols] = w_out[rows, :].T
            return carry

        lax.fori_loop(0, FF // 256, step, 0)

    lane_head = lax.broadcasted_iota(I32, (1, WIDE), 1) // HEAD_DIM
    masks = [(lane_head == h).astype(F32) for h in range(GROUP)]
    masks_low = [m.astype(BF) for m in masks]

    def spread(v):
        return jnp.concatenate([v * mask for mask in masks_low], axis=0)

    def gather_heads(v):
        v = v.reshape(GROUP, ROWS, WIDE)
        return v[0] * masks[0] + v[1] * masks[1] + v[2] * masks[2] + v[3] * masks[3]

    def probs_at(m, g):
        return w_out.at[pl.ds(pl.multiple_of(m * 640, 640), 640), g * WIDE:g * WIDE + ROWS]

    def half_at(part):
        return jnp.where(part // 2 == c, 0, 2), slice((part % 2) * D, (part % 2 + 1) * D)

    def core_slot(core):
        return jnp.where(core == c, 0, 2)

    def attention_forward(m):
        rows = rows_of(m)

        @pl.when(sec > 0)
        def _():
            forward_copy(m).wait_recv()

        xf[...] = xs[m].astype(F32)

        @pl.when(first)
        def _():
            hot = places(m)
            xf[...] += dot(hot, w_out[POS_HI:POS_LO, :]) + dot(hot, w_out[POS_LO:POS_GRAD, :])

        norm(m, rows, xf[...])
        keep_copy("normed", m).start()
        for part in range(3):
            @pl.when(first & (m == 0))
            def _():
                load_in(part).wait()

            cols = slice(part * D, (part + 1) * D)
            proj = dot(a1[0, rows, :], w_in[:, cols])
            if part != 1:
                proj = proj + bi[:, cols].astype(F32)
            slot, at = ((0, D), (2, 0), (2, D))[part]
            a2[slot, rows, at:at + D] = proj.astype(BF)

        @pl.when(first & (m == 0))
        def _():
            load_in(3).wait()

        ends = ends_of(m)
        seg_rows = segment(ends, lax.broadcasted_iota(I32, (ROWS, ROWS), 0))
        seg_cols = segment(ends, lax.broadcasted_iota(I32, (ROWS, ROWS), 1))
        same = seg_rows == seg_cols
        for g in range(D // WIDE):
            lo = D + g * WIDE
            q = spread(a2[0, rows, lo:lo + WIDE])
            k = a2[2, rows, lo - D:lo - D + WIDE]
            v = a2[2, rows, lo:lo + WIDE]
            s = dot_nt(q, k).reshape(GROUP, ROWS, ROWS) * HEAD_DIM ** (-0.5)
            s = jnp.where(same[None], s, MASKED_SCORE)
            s = jnp.exp(s - jnp.max(s, axis=2, keepdims=True))
            p = s * (1.0 / jnp.sum(s, axis=2, keepdims=True))
            p = p.reshape(GROUP * ROWS, ROWS).astype(BF)
            probs_at(m, g)[...] = p
            a2[0, rows, g * WIDE:(g + 1) * WIDE] = gather_heads(dot(p, v)).astype(BF)
        keep_copy("mixed", m).start()
        finish_forward(m, dot(a2[0, rows, 0:D], w_in[:, 3 * D:4 * D]) + bias_out)

    def attention_backward(m):
        rows = rows_of(m)
        backward_copy(m).wait_recv()
        d = ds[0, m]
        slot, cols = half_at(3)
        gs[slot, rows, cols] = d
        vec[0:1, :] += col_sum(d.astype(F32))
        d_mixed = dot(d, w_in_t[3 * D:4 * D, :]).astype(BF)
        for g in range(D // WIDE):
            lo = D + g * WIDE
            q = spread(a2[0, rows, lo:lo + WIDE])
            k = a2[2, rows, lo - D:lo - D + WIDE]
            v = a2[2, rows, lo:lo + WIDE]
            dm = spread(d_mixed[:, g * WIDE:(g + 1) * WIDE])
            p = probs_at(m, g)[...]
            dp_ = dot_nt(dm, v)
            pf = p.astype(F32)
            row_dot = jnp.sum(pf * dp_, axis=1, keepdims=True)
            d_s = (pf * (dp_ - row_dot)).astype(BF)
            dq = (gather_heads(dot(d_s, k)) * HEAD_DIM ** (-0.5)).astype(BF)
            dk = (dot_tn(d_s, q) * HEAD_DIM ** (-0.5)).astype(BF)
            dv = dot_tn(p, dm).astype(BF)
            low = slice(g * WIDE, (g + 1) * WIDE)
            high = slice(D + g * WIDE, D + (g + 1) * WIDE)
            gs[half_at(0)[0], rows, low] = dq
            gs[half_at(1)[0], rows, high] = dk
            gs[half_at(2)[0], rows, low] = dv
            vec_in[0:1, low] += col_sum(dq.astype(F32))
            vs = slice(2 * D + g * WIDE, 2 * D + (g + 1) * WIDE)
            vec_in[0:1, vs] += col_sum(dv.astype(F32))
        keep_copy("inner", m).start()
        d_normed = dot(gs[half_at(0)[0], rows, :], w_in_t[0:2 * D, :])
        d_normed = d_normed + dot(gs[half_at(2)[0], rows, 0:D], w_in_t[2 * D:3 * D, :])
        finish_backward(m, norm_back(m, rows, d_normed, d.astype(F32)))

        @pl.when(first)
        def _():
            at = pl.ds(pl.multiple_of(POS_GRAD + m * KINDS, KINDS), KINDS)
            w_out[at, :] = dot_tn(places(m), xo[m]).astype(BF)

    def hidden_in(rows, part):
        cols = slice(part * D, (part + 1) * D)
        return dot(a1[0, rows, :], w_in[:, cols]) + bi[:, cols].astype(F32)

    def hidden(rows, part, v):
        cdf = 0.5 + 0.5 * lax.erf(v * INV_SQRT2)
        act = (v * cdf).astype(BF)
        for n in range(8):
            chip, core = part * 4 + n // 2, n % 2
            a2[core_slot(core), rows, chip * 128:(chip + 1) * 128] = act[:, n * 128:(n + 1) * 128]
        return act, cdf + v * (INV_SQRT_2PI * jnp.exp(-0.5 * v * v))

    def enter(m, rows):
        forward_copy(m).wait_recv()
        xf[...] = xs[m].astype(F32)
        norm(m, rows, xf[...])
        keep_copy("normed", m).start()

    def second_part(part, act):
        total = None
        for core in (0, 1):
            units = jnp.concatenate(
                [act[:, (2 * n + core) * 128:(2 * n + core + 1) * 128] for n in range(4)], axis=1)
            term = dot(units, w_out[core * HALF + part * 512:core * HALF + (part + 1) * 512, :])
            total = term if total is None else total + term
        return total

    def back_part(part, d_inner):
        return dot(d_inner, w_in_t[part * D:(part + 1) * D, :])

    def leave(m, d, d_normed):
        keep_copy("inner", m).start()
        finish_backward(m, norm_back(m, rows_of(m), d_normed, d.astype(F32)))

    def set_inner(rows, part, d_inner):
        slot, at = half_at(part)
        gs[slot, rows, at] = d_inner
        vec_in[0:1, part * D:(part + 1) * D] += col_sum(d_inner.astype(F32))

    def feed_forward(m):
        rows = rows_of(m)
        enter(m, rows)
        branch, before = bias_out, None
        for part in range(4):
            v = hidden_in(rows, part)
            if before is not None:
                branch = branch + second_part(part - 1, before)
            before, slope = hidden(rows, part, v)
            slot, at = half_at(part)
            gs[slot, rows, at] = slope.astype(BF)
        keep_copy("act", m).start()
        finish_forward(m, branch + second_part(3, before))

    def feed_backward(m):
        rows = rows_of(m)
        backward_copy(m).wait_recv()
        keep_copy("branch", m).start()
        d = ds[0, m]
        vec[0:1, :] += col_sum(d.astype(F32))
        d_normed, before = 0.0, None
        for part in range(4):
            slot, at = half_at(part)
            d_act = dot(d, w_out_t[:, part * D:(part + 1) * D])
            if before is not None:
                d_normed = d_normed + back_part(part - 1, before)
            before = (d_act * gs[slot, rows, at].astype(F32)).astype(BF)
            set_inner(rows, part, before)
        leave(m, d, d_normed + back_part(3, before))

    def last_before(m):
        rows = rows_of(m)
        d = (ds[0, m].astype(F32) * keep_of(m)).astype(BF)
        ds[0, m] = d
        keep_copy("branch", m).start()
        vec[0:1, :] += col_sum(d.astype(F32))

        def step(part, carry):
            slot = jnp.where(part // 2 == c, 0, 2)
            at = pl.ds(pl.multiple_of((part % 2) * D, D), D)
            cols = pl.ds(pl.multiple_of(part * D, D), D)
            gs[slot, rows, at] = dot(d, w_out_t[:, cols]).astype(BF)
            return carry

        lax.fori_loop(0, 4, step, 0)

    def last_both(m):
        rows = rows_of(m)
        enter(m, rows)
        w_out_t[rows, 0:D] = xf[...].astype(BF)
        d_normed, before = 0.0, None
        for part in range(4):
            v = hidden_in(rows, part)
            if before is not None:
                d_normed = d_normed + back_part(part - 1, before)
            slope = hidden(rows, part, v)[1]
            slot, at = half_at(part)
            before = (gs[slot, rows, at].astype(F32) * slope).astype(BF)
            set_inner(rows, part, before)
        leave(m, ds[0, m], d_normed + back_part(3, before))
        keep_copy("act", m).start()

    def last_after(m):
        rows = rows_of(m)
        keep = keep_of(m)

        def step(n, carry):
            cols = pl.ds(pl.multiple_of(n * 512, 512), 512)
            branch = dot(a2[core_slot(0), rows, :], w_out[0:HALF, cols]) + bo[:, cols].astype(F32)
            branch = branch + dot(a2[core_slot(1), rows, :], w_out[HALF:FF, cols])
            out = w_out_t[rows, cols].astype(F32) + branch
            xs[m, :, cols] = out.astype(BF)
            vec[3:4, cols] += col_sum(keep * out * out)
            vec[4:5, cols] += col_sum(keep * branch * branch)
            return carry

        lax.fori_loop(0, 2, step, 0)

    def say_ready():
        for peer in (z_peers[1], z_peers[3], y_peers[1], y_peers[3]):
            pl.semaphore_signal(ready, inc=1, device_id=peer, device_id_type=MESH)


    coords = ((z, y), (y, z), (z, y))
    peers = ((z_peers, y_peers), (y_peers, z_peers), (z_peers, y_peers))
    sets = (0, 1, 2)

    def start_small(height):
        def cross():
            return remote(small.at[:, :, other, 0:height], small_x.at[:, :, 0:height], o_send.at[2],
                          o_recv.at[2], sibling)

        count = jnp.int32(0)
        for k in (1, 2, 3):
            stat_copy(k).wait_recv()
        for j in range(32):
            quad = slice((j // 4) * 128, (j // 4 + 1) * 128)
            at = (j // 8, (j // 2) % 4, j % 2)
            small[at + (slice(0, 1),)] = vec_in[0:1, j * 128:(j + 1) * 128]
            small[at + (slice(1, 4),)] = vec[0:3, quad]
            for s in range(4):
                small[at + (slice(4 + s, 5 + s),)] = stat_s[s, 0:1, :]
        cross().start()
        return cross

    def reduce(block_of, land1_of, land2_of, half, height, make, between):
        def block(s, a, b):
            return small_sum.at[a, b, 0:height] if s == 2 else block_of(s, a, b)

        def land1(s, i, q):
            return small_1.at[i, q, 0:height] if s == 2 else land1_of(s, i, q)

        def land2(s, i):
            return small_2.at[i, 0:height // 2] if s == 2 else land2_of(s, i)

        def target(p, i):
            return {0: (plus(p, 2), 0), 1: (plus(p, 2), 1), 2: (plus(p, 1), 1),
                    3: (plus(p, 3), 0), 4: (plus(p, 1), 0), 5: (plus(p, 3), 1)}[i]

        def step1(s, i, q):
            a, h = target(coords[s][0], i)
            peer = peers[s][0][1 if i % 2 == 0 else 3]
            return remote(block(s, a, 2 * h + q), land1(s, i, q), s1_send.at[s, i, q],
                          s1_recv.at[s, i, q], peer)

        def half_of(s, b, h):
            return block(s, coords[s][0], b).at[h * half[s]:(h + 1) * half[s], :]

        def step2(s, i):
            b, h = target(coords[s][1], i)
            peer = peers[s][1][1 if i % 2 == 0 else 3]
            return remote(half_of(s, b, h), land2(s, i), s2_send.at[s, i], s2_recv.at[s, i], peer)

        def turn_of(s, h, n):
            high, low = coords[s][1] // 2, coords[s][1] % 2
            early = jnp.where(h == high, 1 - low, low)
            return early if n == 0 else 1 - early

        def wait1(s, i, q):
            remote(block(s, 0, 0), land1(s, i, q), s1_send.at[s, i, q], s1_recv.at[s, i, q],
                   sibling).wait_recv()

        def add(ref, *others):
            total = ref[...].astype(F32)
            for o in others:
                total = total + o[...].astype(F32)
            ref[...] = total.astype(ref.dtype)

        cross = start_small(height)
        def start(s, pieces):
            for k in (0, 1):
                for i in pieces:
                    step1(s, i, turn_of(s, target(0, i)[1], k)).start()

        def chunk(t, carry):
            n = jnp.where(t == 0, 2, jnp.where(t == 1, 1, jnp.where(t == 2, 3, 0)))
            for s in (0, 1):
                make(s, plus(coords[s][0], n))
                if s == 0:
                    @pl.when(t == 0)
                    def _():
                        pl.semaphore_wait(ready, 4)
                        cross().wait_recv()
                        small_sum[:, :, 0:height] = (
                            small[:, :, c, 0:height] + small_x[:, :, 0:height])
                        start(2, (0, 1, 2, 3))
                for when, pieces in ((0, (0, 1)), (1, (2,)), (2, (3,))):
                    @pl.when(t == when)
                    def _():
                        start(s, pieces)
            return carry

        lax.fori_loop(0, 4, chunk, 0)
        for k in (0, 1):
            for i in (4, 5):
                for s in (2, 0, 1):
                    a, h = target(coords[s][0], i)
                    q = turn_of(s, h, k)
                    step1(s, i - 4, q).wait_recv()
                    add(block(s, a, 2 * h + q), land1(s, i - 4, q))
                    step1(s, i, q).start()
        between()
        for n, pieces in ((2, (0, 1)), (1, (2,)), (3, (3,)), (0, ())):
            for s in sets:
                p1, p2 = coords[s]
                b = plus(p2, n)
                h, q = b // 2, b % 2
                up, down = jnp.where(h == 0, 4, 2), jnp.where(h == 0, 3, 5)
                wait1(s, up, q)
                wait1(s, down, q)
                add(block(s, p1, b), land1(s, up, q), land1(s, down, q))
                for i in pieces:
                    step2(s, i).start()
        for i in (4, 5):
            for s in sets:
                b, h = target(coords[s][1], i)
                step2(s, i - 4).wait_recv()
                add(half_of(s, b, h), land2(s, i - 4))
                step2(s, i).start()
        for s in sets:
            p2 = coords[s][1]
            for h, up, down in ((0, 4, 3), (1, 2, 5)):
                step2(s, up).wait_recv()
                step2(s, down).wait_recv()
                add(half_of(s, p2, h), land2(s, up), land2(s, down))
        small_o[...] = small_sum[z, y, 0:8]

        def finish():
            cross().wait_send()
            for s in sets:
                for i in range(6):
                    for q in (0, 1):
                        step1(s, i, q).wait_send()
                    step2(s, i).wait_send()

        return finish

    def stat_copy(k):
        return remote(stat_s.at[sec], stat_s.at[sec], x_send.at[k - 1], x_recv.at[k - 1],
                      x_peers[k])

    def send_stats():
        count = jnp.int32(0)
        for m in range(MICRO):
            count = count + ends_of(m)[2]
        lanes = lax.broadcasted_iota(I32, (8, 128), 1)
        stream_sq = jnp.sum(vec[3:4, :], axis=1, keepdims=True)
        branch_sq = jnp.sum(vec[4:5, :], axis=1, keepdims=True)
        stat_s[sec] = jnp.where(
            lanes == 0, stream_sq,
            jnp.where(lanes == 1, branch_sq, jnp.where(lanes == 2, count.astype(F32), 0.0)))
        for k in (1, 2, 3):
            stat_copy(k).start()

    def both(ref, start, width, *cols):
        return ref[:, :, pl.ds(pl.multiple_of(start, width), width)].reshape(2 * ALL, width).T

    def kept(n):
        for m in range(MICRO):
            keep_copy(n, m).wait_recv()

    def kept_sent(n):
        for m in range(MICRO):
            keep_copy(n, m).wait_send()

    def pos_copy(k):
        return remote(pos_s, pos_s, x_send.at[2 + k], x_recv.at[3], x_peers[k])

    def own_copy(n, src, dst):
        return remote(src, dst, o_send.at[n], o_recv.at[n], sibling)

    @pl.when(first)
    def _():
        build_blend()
        high, low = split(blend[0:SHORT, :])
        rows = dot_tn(high, table[...]) + dot_tn(low, table[...])
        w_out[POS_HI:POS_LO, :], w_out[POS_LO:POS_GRAD, :] = split(rows)
        load_x.wait()

    pl.semaphore_wait(barrier, len(partners))

    @pl.when(is_att)
    def _():
        @pl.when(sec > 0)
        def _():
            for part in range(4):
                load_in(part).wait()
            transpose_in()

        def turn_second():
            kept("normed")
            kept("mixed")

            def step(zz, carry):
                at = pl.ds(pl.multiple_of(zz * 256, 256), 256)
                w_out_t[at, 2 * D:2 * D + 2 * ALL] = jnp.where(
                    c == 0, both(a1, zz * 256, 256), both(a2.at[0:2], zz * 256, 256))
                return carry

            lax.fori_loop(0, 4, step, 0)

        def tick(t, carry):
            early = (sec == 2) & (t == MICRO - 1)
            late = (sec == 2) & (t == MICRO)
            is_fwd = ((t < MICRO) & jnp.logical_not(early)) | late
            m = jnp.where(early, 0, jnp.where(late, MICRO - 1, t % MICRO))

            @pl.when(is_fwd)
            def _():
                attention_forward(m)

            @pl.when(is_fwd & (m == MICRO - 1))
            def _():
                @pl.when(first)
                def _():
                    transpose_in()

                send_stats()
                say_ready()

                @pl.when(first)
                def _():
                    turn_second()

            @pl.when(jnp.logical_not(is_fwd))
            def _():
                attention_backward(m)

            return carry

        lax.fori_loop(0, 2 * MICRO, tick, 0)

        @pl.when(first)
        def _():
            own_edge(0, input_s).start()

        @pl.when(sec > 0)
        def _():
            turn_second()

        kept("inner")

        def block(s, a, b):
            zz, yy = (a, b) if s == 0 else (b, a)
            at = pl.ds(pl.multiple_of(zz * 256 + yy * 64, 64), 64)
            return w_out_t.at[at, s * D:(s + 1) * D]

        def land1(s, i, q):
            at = pl.ds(pl.multiple_of((i * 2 + q) * 64, 64), 64)
            return w_in.at[at, s * HALF:s * HALF + D]

        def land2(s, i):
            return w_in.at[768 + i * 32:768 + (i + 1) * 32, s * HALF:s * HALF + D]

        def make(s, a):
            if s == 1:
                lhs = jnp.concatenate([
                    w_out_t[pl.ds(pl.multiple_of(zz * 256 + a * 64, 64), 64), 2 * D:2 * D + 2 * ALL]
                    for zz in range(4)], axis=0)
                rhs = gs[0:2, :, D:2 * D].reshape(2 * ALL, D)
                made = dot(lhs, rhs).astype(BF)
                for zz in range(4):
                    w_out_t[pl.ds(pl.multiple_of(zz * 256 + a * 64, 64), 64), D:2 * D] = (
                        made[zz * 64:(zz + 1) * 64, :])
            else:
                at = pl.ds(pl.multiple_of(a * 256, 256), 256)
                lhs = both(a1, a * 256, 256)
                rhs = gs[0:2, :, 0:D].reshape(2 * ALL, D)
                w_out_t[at, 0:D] = dot(lhs, rhs).astype(BF)

        small[...] = jnp.zeros_like(small)

        @pl.when(first)
        def _():
            total = jnp.zeros((128, D), F32)
            grads = w_out[POS_GRAD:POS_GRAD + MICRO * KINDS, :].reshape(MICRO, KINDS, D)
            b_hi, b_lo = split(blend[...])
            for m in range(MICRO):
                total = total + dot(b_hi, grads[m]) + dot(b_lo, grads[m])
            for pair in (0, 1):
                both_sections = jnp.concatenate(
                    [total[0:64, (2 * pair + n) * 256:(2 * pair + n + 1) * 256] for n in (0, 1)],
                    axis=0)
                at = slice(8 + pair * 8, 16 + pair * 8)
                small[:, :, :, at] = both_sections.T.reshape(4, 4, 2, 8, 128)

        finish = reduce(block, land1, land2, (32, 32, 16), 32, make, lambda: None)

        def sent(n):
            return block(n, coords[n][0], coords[n][1]).at[
                pl.ds(pl.multiple_of(other * 32, 32), 32), :]

        def mine(n):
            return block(n, coords[n][0], coords[n][1]).at[
                pl.ds(pl.multiple_of(c * 32, 32), 32), :]

        def swap(n):
            return own_copy(n, sent(n), got_in.at[:, n * D:(n + 1) * D])

        for n in (0, 1):
            swap(n).start()

        @pl.when(first)
        def _():
            pos_s[...] = small_sum[z, y, 8:24]
            for k in (1, 2, 3):
                pos_copy(k).start()

        for n in (0, 1):
            swap(n).wait_recv()
        copies = [
            pltpu.make_async_copy(mine(n), gin_o.at[c, :, n * D:(n + 1) * D], out_sem.at[n])
            for n in (0, 1)]
        copies.append(pltpu.make_async_copy(got_in, gin_o.at[other], out_sem.at[2]))
        for copy in copies:
            copy.start()
        finish()
        for n in (0, 1):
            swap(n).wait_send()
        for copy in copies:
            copy.wait()
        kept_sent("normed")
        kept_sent("mixed")
        kept_sent("inner")

    @pl.when(is_ff)
    def _():
        for part in range(4):
            load_in(part).wait()

        def arrived(n, carry):
            load_out(n).wait()
            return carry

        lax.fori_loop(0, 32, arrived, 0)

        def each(work):
            def step(m, carry):
                work(m)
                return carry

            lax.fori_loop(0, MICRO, step, 0)

        @pl.when(last)
        def _():
            load_d.wait()
            transpose_out()
            transpose_in()
            each(last_before)
            each(last_both)
            each(last_after)

        @pl.when(jnp.logical_not(last))
        def _():
            each(feed_forward)
            transpose_out()
            transpose_in()

        say_ready()
        send_stats()

        @pl.when(jnp.logical_not(last))
        def _():
            each(feed_backward)

        for n in ("normed", "act", "branch", "inner"):
            kept(n)

        def block(s, a, b):
            if s == 0:
                at = pl.ds(pl.multiple_of(a * 256 + b * 64, 64), 64)
                return w_out_t.at[at, 0:HALF]
            at = pl.ds(pl.multiple_of(b * 512 + a * 128, 128), 128)
            return w_in_t.at[at, :]

        def land1(s, i, q):
            n = i * 2 + q
            if s == 0:
                return w_in.at[pl.ds(pl.multiple_of(n * 64, 64), 64), 0:HALF]
            rows = pl.ds(pl.multiple_of((n % 8) * 128, 128), 128)
            return w_in.at[rows, pl.ds(pl.multiple_of(HALF + (n // 8) * D, D), D)]

        def land2(s, i):
            if s == 0:
                return w_in.at[768 + i * 32:768 + (i + 1) * 32, 0:HALF]
            return w_in.at[512 + i * 64:512 + (i + 1) * 64, FF - D:FF]

        def make(s, a):
            if s == 0:
                at = pl.ds(pl.multiple_of(a * 256, 256), 256)
                lhs = both(a1, a * 256, 256)
                for n in (0, 1):
                    cols = slice(n * D, (n + 1) * D)
                    rhs = gs[0:2, :, cols].reshape(2 * ALL, D)
                    w_out_t[at, cols] = dot(lhs, rhs).astype(BF)
            else:
                def step(pair, carry):
                    lhs = []
                    for n in (0, 1):
                        chip = (pair * 2 + n) * 4 + a
                        lhs.append(both(a2.at[0:2], chip * 128, 128))
                    rhs = ds[...].reshape(2 * ALL, D)
                    block2 = dot(jnp.concatenate(lhs, axis=0), rhs).astype(BF)
                    for n in (0, 1):
                        chip = (pair * 2 + n) * 4 + a
                        at = pl.ds(pl.multiple_of(chip * 128, 128), 128)
                        w_in_t[at, :] = block2[n * 128:(n + 1) * 128, :]
                    return carry

                lax.fori_loop(0, 2, step, 0)

        small[...] = jnp.zeros_like(small)
        def between():
            @pl.when(last)
            def _():
                for k in (1, 2, 3):
                    layer_copy(k).start()
                own_edge(3, layer_s).start()

        finish = reduce(block, land1, land2, (32, 64, 8), 16, make, between)

        def part(core):
            return block(0, z, y).at[pl.ds(pl.multiple_of(core * 32, 32), 32), :]

        swap = own_copy(0, part(other), got_in)
        swap.start()
        swap.wait_recv()
        copies = [
            pltpu.make_async_copy(src, dst, out_sem.at[n]) for n, (src, dst) in enumerate((
                (part(c), gin_o.at[c]), (got_in, gin_o.at[other]), (block(1, y, z), gout_o)))]
        for copy in copies:
            copy.start()
        finish()
        swap.wait_send()
        for copy in copies:
            copy.wait()
        for n in ("normed", "act", "branch", "inner"):
            kept_sent(n)

    @pl.when(first)
    def _():
        own_edge(0, input_s).wait()
        layer_copy(1).wait_recv()

    @pl.when(sec > 0)
    def _():
        for m in range(MICRO):
            input_copy(1, m).wait_recv()

        @pl.when(sec < 3)
        def _():
            layer_copy(1).wait_recv()

        @pl.when(last)
        def _():
            own_edge(3, layer_s).wait()

    outs = [pltpu.make_async_copy(layer_s, layer_o, out_sem.at[3]),
            pltpu.make_async_copy(input_s, input_o, out_sem.at[4])]
    for copy in outs:
        copy.start()

    @pl.when(sec > 0)
    def _():
        pos_copy(1).wait_recv()

        for m in range(MICRO):
            backward_copy(m).wait_send()

    gpos_o[...] = pos_s[...]
    for k in (1, 2, 3):
        stat_copy(k).wait_send()

    @pl.when(first)
    def _():
        for k in (1, 2, 3):
            pos_copy(k).wait_send()
            for m in range(MICRO):
                input_copy(k, m).wait_send()

    @pl.when(last)
    def _():
        for k in (1, 2, 3):
            layer_copy(k).wait_send()

    for copy in outs:
        copy.wait()


def output_kernel(
    layer, inp, gin, gout, small, gpos,
    layer_o, input_o, gin_o, gout_o, bin_o, bout_o, gain_o, shift_o, pos_o, stats_o,
):
    sec = lax.axis_index("section")
    quarter = lax.axis_index("dp") % 4
    layer_o[...] = layer[...]
    input_o[...] = inp[...]
    for half in (0, 1):
        gin_o[0, :, half * HALF:(half + 1) * HALF] = gin[half].astype(F32)

    @pl.when(sec % 2 == 0)
    def _():
        gout_o[...] = jnp.zeros_like(gout_o)

    @pl.when(sec % 2 == 1)
    def _():
        gout_o[0] = gout[...].astype(F32)

    bin_o[...] = small[0:1, :]
    for row, ref in ((1, bout_o), (2, gain_o), (3, shift_o)):
        line = small[row:row + 1, :]
        picked = line[:, 0:32]
        for n in (1, 2, 3):
            picked = jnp.where(quarter == n, line[:, n * 32:(n + 1) * 32], picked)
        ref[...] = picked
    pair = jnp.where(sec < 2, gpos[0:8, :], gpos[8:16, :])
    pos_o[...] = jnp.where(sec % 2 == 0, pair[:, 0:SHORT], pair[:, 64:64 + SHORT])
    count = small[4:5, 2:3]
    kind = lax.broadcasted_iota(I32, (2, 4), 0)
    section = lax.broadcasted_iota(I32, (2, 4), 1)
    total = jnp.zeros((2, 4), F32)
    for s in range(4):
        for r in range(2):
            total = jnp.where(
                (kind == r) & (section == s), small[4 + s:5 + s, r:r + 1], total)
    stats_o[...] = jnp.sqrt(total / (count * D))


def local(inputs, cotangent, layout, pos_index, pos_table, slab_in, slab_out, bias_in, bias_out,
          ln_gain, ln_bias):
    shape = jax.ShapeDtypeStruct
    vmem = pl.BlockSpec(memory_space=pltpu.VMEM)
    smem = pl.BlockSpec(memory_space=pltpu.SMEM)
    anywhere = pl.BlockSpec(memory_space=pl.ANY)
    dma = pltpu.SemaphoreType.DMA

    parts = pl.pallas_call(
        train_kernel,
        name="train",
        out_shape=(
            shape((MICRO, ROWS, 256), BF), shape((MICRO, ROWS, 256), BF), shape((2, 32, HALF), BF), shape((128, D), BF),
            shape((8, 128), F32), shape((16, 128), F32)),
        in_specs=[smem] + [anywhere] * 4 + [vmem] * 6,
        out_specs=(anywhere,) * 4 + (vmem,) * 2,
        scratch_shapes=[
            pltpu.VMEM((D, FF), BF), pltpu.VMEM((FF, D), BF),
            pltpu.VMEM((FF, D), BF), pltpu.VMEM((D, FF), BF),
            pltpu.VMEM((MICRO, ROWS, D), BF), pltpu.VMEM((2, MICRO, ROWS, D), BF),
            pltpu.VMEM((MICRO, ROWS, D), BF),
            pltpu.VMEM((2, ALL, D), BF), pltpu.VMEM((3, ALL, HALF), BF),
            pltpu.VMEM((3, ALL, HALF), BF),
            pltpu.VMEM((ROWS, 128), F32), pltpu.VMEM((ROWS, D), F32),
            pltpu.VMEM((8, FF), F32), pltpu.VMEM((8, D), F32), pltpu.VMEM((128, KINDS), F32),
            pltpu.VMEM((32, HALF), BF),
            pltpu.VMEM((4, 4, 2, 32, 128), F32), pltpu.VMEM((4, 4, 32, 128), F32),
            pltpu.VMEM((4, 4, 32, 128), F32), pltpu.VMEM((6, 2, 32, 128), F32),
            pltpu.VMEM((6, 16, 128), F32), pltpu.VMEM((4, 8, 128), F32),
            pltpu.VMEM((16, 128), F32),
            pltpu.VMEM((MICRO, ROWS, 256), BF), pltpu.VMEM((MICRO, ROWS, 256), BF),
            dma((6,)), dma((32,)), dma((MICRO,)), dma((MICRO,)), dma((MICRO,)), dma((MICRO,)),
            dma((4, MICRO)), dma((4, MICRO)), pltpu.SemaphoreType.REGULAR,
            dma((3, 6, 2)), dma((3, 6, 2)), dma((3, 6)), dma((3, 6)), dma((3,)), dma((3,)),
            dma((6,)), dma((4,)), dma((3,)), dma((3, MICRO)), dma((MICRO + 1,)), dma((1,)), dma((5,)),
        ],
        compiler_params=pltpu.CompilerParams(
            collective_id=0, has_side_effects=True, vmem_limit_bytes=64 * MIB - 65536),
    )(layout.transpose(2, 1, 0), inputs, cotangent, slab_in, slab_out, bias_in, bias_out, ln_gain,
      ln_bias, pos_index.T, pos_table)

    *grads, grad_pos, stats = pl.pallas_call(
        output_kernel,
        name="outputs",
        out_shape=(
            shape((MICRO, ROWS, 256), BF), shape((MICRO, ROWS, 256), BF), shape((1, 32, FF), F32),
            shape((1, 128, D), F32), shape((1, 128), F32), shape((1, 32), F32),
            shape((1, 32), F32), shape((1, 32), F32), shape((8, SHORT), F32), shape((2, 4), F32)),
        in_specs=[vmem] * 6,
        out_specs=(vmem,) * 10,
        compiler_params=pltpu.CompilerParams(vmem_limit_bytes=60 * MIB),
    )(*parts)
    return (*grads, grad_pos.T, stats)


def solution(mesh):
    return jax.shard_map(
        local,
        mesh=mesh,
        in_specs=(
            P(None, "dp", None), P(None, "dp", None), P(None, "dp", None), P(), P(),
            P("section", None, None), P("section", None, None), P("section", None),
            P("section", None), P("section", None), P("section", None)),
        out_specs=(
            P(None, "dp", "section"), P(None, "dp", "section"), P("section", "dp", None),
            P("section", "dp", None), P("section", "dp"), P("section", "dp"),
            P("section", "dp"), P("section", "dp"), P(None, ("section", "dp")), P()),
        check_vma=False,
    )
```

```python
import jax
import jax.numpy as jnp
from jax import lax
from jax.experimental import pallas as pl
from jax.experimental.pallas import tpu as pltpu
from jax.sharding import PartitionSpec as P

BF = jnp.bfloat16
F32 = jnp.float32
I32 = jnp.int32
MESH = pl.DeviceIdType.MESH

D = 1024
FF = 4096
HALF = FF // 2
HEAD_DIM = 64
SHORT = 50
LONG = 145
MICRO = 4
ROWS = 160
ALL = MICRO * ROWS
SLOTS = 3
GROUP = 4
WIDE = GROUP * HEAD_DIM
KINDS = 256
CORNERS = 4
LN_EPSILON = 1e-06
MASKED_SCORE = -1e30
INV_SQRT2 = 0.7071067811865476
INV_SQRT_2PI = 0.3989422804014327
MIB = 2**20
POS_HI = MICRO * GROUP * ROWS
POS_LO = POS_HI + KINDS
POS_GRAD = POS_LO + KINDS


def dot(a, b):
    return lax.dot_general(a, b, (((1,), (0,)), ((), ())), preferred_element_type=F32)


def dot_nt(a, b):
    return lax.dot_general(a, b, (((1,), (1,)), ((), ())), preferred_element_type=F32)


def dot_tn(a, b):
    return lax.dot_general(a, b, (((0,), (0,)), ((), ())), preferred_element_type=F32)


def split(v):
    high = v.astype(BF)
    return high, (v - high.astype(F32)).astype(BF)


def col_sum(v):
    return jnp.sum(v, axis=0, keepdims=True)


def train_kernel(
    lay, inp, cot, slab_in, slab_out, bi, bo, ga, sh, index, table,
    layer_o, input_o, gin_o, gout_o, small_o, gpos_o,
    w_in, w_out, w_in_t, w_out_t, xs, ds, xo, a1, gs, a2, rstd, xf, vec_in, vec, blend, got_in,
    small, small_x, small_sum, small_1, small_2, stat_s, pos_s, layer_s, input_s,
    load_sem, out_load, f_send, f_recv, b_send, b_recv, k_send, k_recv, ready,
    s1_send, s1_recv, s2_send, s2_recv, o_send, o_recv, x_send, x_recv, e_send, i_send, e_recv, own_sem,
    out_sem,
):
    sec = lax.axis_index("section")
    dp = lax.axis_index("dp")
    z, y, c = dp // 8, (dp // 2) % 4, dp % 2
    other = 1 - c
    is_att = sec % 2 == 0
    is_ff = jnp.logical_not(is_att)
    first = sec == 0
    last = sec == 3

    def plus(v, k):
        return lax.rem(v + k, 4)

    def at_dp(zz, yy, cc):
        return {"dp": (zz * 4 + yy) * 2 + cc}

    sibling = at_dp(z, y, other)
    z_peers = {k: at_dp(plus(z, k), y, c) for k in (1, 2, 3)}
    y_peers = {k: at_dp(z, plus(y, k), c) for k in (1, 2, 3)}
    x_peers = {k: {"section": plus(sec, k)} for k in (1, 2, 3)}

    def z_near(k, core):
        return at_dp(plus(z, k), y, core)

    def y_near(k, core):
        return at_dp(z, plus(y, k), core)

    across = [near(k, other) for near in (z_near, y_near) for k in (1, 3)]

    def remote(src, dst, send, recv, device):
        return pltpu.make_async_remote_copy(
            src_ref=src, dst_ref=dst, send_sem=send, recv_sem=recv, device_id=device,
            device_id_type=MESH)

    load_x = pltpu.make_async_copy(inp, xs, load_sem.at[4])
    load_d = pltpu.make_async_copy(cot, ds.at[0], load_sem.at[5])

    def load_out(n):
        return pltpu.make_async_copy(
            slab_out.at[0, pl.ds(pl.multiple_of(n * 128, 128), 128)],
            w_out.at[pl.ds(pl.multiple_of((n % 2) * HALF + (n // 2) * 128, 128), 128)],
            out_load.at[n])

    def load_in(part):
        cols = slice(part * D, (part + 1) * D)
        return pltpu.make_async_copy(slab_in.at[0, :, cols], w_in.at[:, cols], load_sem.at[part])

    @pl.when(first)
    def _():
        load_x.start()

    for part in range(4):
        load_in(part).start()

    @pl.when(is_ff)
    def _():
        def start(n, carry):
            load_out(n).start()
            return carry

        lax.fori_loop(0, 32, start, 0)

    @pl.when(last)
    def _():
        load_d.start()

    barrier = pltpu.get_barrier_semaphore()
    partners = [sibling] + [peers[k] for peers in (x_peers, y_peers, z_peers) for k in (1, 2, 3)]
    partners += across
    for partner in partners:
        pl.semaphore_signal(barrier, inc=1, device_id=partner, device_id_type=MESH)

    vec_in[...] = jnp.zeros_like(vec_in)
    vec[...] = jnp.zeros_like(vec)
    rstd[...] = jnp.zeros_like(rstd)
    gain = ga[...].astype(F32)
    shift = sh[...].astype(F32)
    bias_out = bo[...].astype(F32)

    def forward_copy(m):
        return remote(xo.at[m], xs.at[m], f_send.at[m], f_recv.at[m], x_peers[1])

    def backward_copy(m):
        return remote(xo.at[m], ds.at[0, m], b_send.at[m], b_recv.at[m], x_peers[3])

    def rows_of(m):
        return pl.ds(pl.multiple_of(m * ROWS, ROWS), ROWS)

    def keep_copy(kind, m):
        rows = rows_of(m)
        if kind == "normed":
            n, src, dst = 0, a1.at[0, rows], a1.at[1, rows]
        elif kind == "act":
            n, src, dst = 1, a2.at[2, rows], a2.at[1, rows]
        elif kind == "mixed":
            n, src, dst = 1, a2.at[0, rows, 0:D], a2.at[1, rows, 0:D]
        elif kind == "inner":
            n, src, dst = 2, gs.at[2, rows], gs.at[1, rows]
        else:
            n, src, dst = 3, ds.at[0, m], ds.at[1, m]
        return remote(src, dst, k_send.at[n, m], k_recv.at[n, m], sibling)

    def columns(ref, s):
        return ref.at[:, :, pl.ds(pl.multiple_of(s * 256, 256), 256)]

    def layer_copy(k):
        return remote(columns(xs, plus(sec, k)), layer_s, e_send.at[k - 1], e_recv.at[MICRO],
                      x_peers[k])

    def input_copy(k, m):
        at = pl.ds(pl.multiple_of(plus(sec, k) * 256, 256), 256)
        return remote(xo.at[m, :, at], input_s.at[m], i_send.at[k - 1, m], e_recv.at[m], x_peers[k])

    def own_edge(s, landing):
        return pltpu.make_async_copy(columns(xo if s == 0 else xs, s), landing, own_sem.at[0])

    def ends_of(m):
        ends, total = [], jnp.int32(0)
        for k in range(SLOTS):
            kind = lay[k, 0, m]
            total = total + jnp.where(kind == 1, SHORT, jnp.where(kind == 2, LONG, 0))
            ends.append(total)
        return ends

    def segment(ends, ids):
        return jnp.where(
            ids < ends[0], 0, jnp.where(ids < ends[1], 1, jnp.where(ids < ends[2], 2, -1)))

    def keep_of(m):
        ends = ends_of(m)
        return (lax.broadcasted_iota(I32, (ROWS, 1), 0) < ends[2]).astype(F32)

    def places(m):
        ends = ends_of(m)
        ids = lax.broadcasted_iota(I32, (ROWS, 1), 0)
        starts = [jnp.int32(0), ends[0], ends[1]]
        place = jnp.full((ROWS, 1), -1, I32)
        for k in range(SLOTS):
            offset = ids - starts[k]
            blended = (lay[k, 0, m] == 2) & (offset >= 1)
            kind = jnp.where(blended, offset - 1, offset + (LONG - 1))
            place = jnp.where((offset >= 0) & (ids < ends[k]), kind, place)
        return (place == lax.broadcasted_iota(I32, (ROWS, KINDS), 1)).astype(F32).astype(BF)

    def build_blend():
        blend[0:8, :] = jnp.full((8, KINDS), -1.0, F32)
        blend[0:CORNERS, 0:LONG - 1] = index[...].astype(F32)
        ids = blend[0:8, :]
        t = lax.broadcasted_iota(I32, (128, KINDS), 0)
        kind = lax.broadcasted_iota(I32, (128, KINDS), 1)
        tf = t.astype(F32)
        total = jnp.where((kind - (LONG - 1) == t) & (t < SHORT), 1.0, 0.0)
        for corner in range(CORNERS):
            weight = (CORNERS - corner) / (CORNERS * (CORNERS + 1) / 2.0)
            total = total + jnp.where(ids[corner:corner + 1, :] == tf, weight, 0.0)
        blend[...] = total

    def norm(m, rows, x):
        mean = jnp.mean(x, axis=1, keepdims=True)
        centered = x - mean
        variance = jnp.mean(centered * centered, axis=1, keepdims=True)
        scale = lax.rsqrt(variance + LN_EPSILON)
        hat = centered * scale
        lane = lax.broadcasted_iota(I32, (ROWS, 128), 1)
        rstd[...] = jnp.where(lane == m, scale, rstd[...])
        xs[m] = hat.astype(BF)
        a1[0, rows, :] = (hat * gain + shift).astype(BF)

    def norm_back(m, rows, d_normed, d):
        hat = xs[m].astype(F32)
        vec[1:2, :] += col_sum(d_normed * hat)
        vec[2:3, :] += col_sum(d_normed)
        e = gain * d_normed
        mean_e = jnp.mean(e, axis=1, keepdims=True)
        mean_eh = jnp.mean(e * hat, axis=1, keepdims=True)
        lane = lax.broadcasted_iota(I32, (ROWS, 128), 1)
        scale = jnp.sum(jnp.where(lane == m, rstd[...], 0.0), axis=1, keepdims=True)
        return d + scale * (e - mean_e - hat * mean_eh)

    def add_stats(m, out, branch):
        keep = keep_of(m)
        vec[3:4, :] += col_sum(keep * out * out)
        vec[4:5, :] += col_sum(keep * branch * branch)

    def finish_forward(m, branch):
        out = xf[...] + branch
        xo[m] = out.astype(BF)
        forward_copy(m).start()
        add_stats(m, out, branch)

    def finish_backward(m, d_prev):
        @pl.when(sec < 3)
        def _():
            forward_copy(m).wait_send()

        xo[m] = d_prev.astype(BF)

        @pl.when(sec > 0)
        def _():
            backward_copy(m).start()

        @pl.when(first)
        def _():
            for k in (1, 2, 3):
                input_copy(k, m).start()

    def transpose_in():
        def step(i, carry):
            cols = pl.ds(pl.multiple_of(i * 256, 256), 256)
            w_in_t[cols, :] = w_in[:, cols].T
            return carry

        lax.fori_loop(0, FF // 256, step, 0)

    def transpose_out():
        def step(i, carry):
            for core in (0, 1):
                cols = pl.ds(pl.multiple_of(i * 256 + core * 128, 128), 128)
                rows = pl.ds(pl.multiple_of(core * HALF + i * 128, 128), 128)
                w_out_t[:, cols] = w_out[rows, :].T
            return carry

        lax.fori_loop(0, FF // 256, step, 0)

    lane_head = lax.broadcasted_iota(I32, (1, WIDE), 1) // HEAD_DIM
    masks = [(lane_head == h).astype(F32) for h in range(GROUP)]
    masks_low = [m.astype(BF) for m in masks]

    def spread(v):
        return jnp.concatenate([v * mask for mask in masks_low], axis=0)

    def gather_heads(v):
        v = v.reshape(GROUP, ROWS, WIDE)
        return v[0] * masks[0] + v[1] * masks[1] + v[2] * masks[2] + v[3] * masks[3]

    def probs_at(m, g):
        return w_out.at[pl.ds(pl.multiple_of(m * 640, 640), 640), g * WIDE:g * WIDE + ROWS]

    def half_at(part):
        return jnp.where(part // 2 == c, 0, 2), slice((part % 2) * D, (part % 2 + 1) * D)

    def core_slot(core):
        return jnp.where(core == c, 0, 2)

    def attention_forward(m):
        rows = rows_of(m)

        @pl.when(sec > 0)
        def _():
            forward_copy(m).wait_recv()

        xf[...] = xs[m].astype(F32)

        @pl.when(first)
        def _():
            hot = places(m)
            xf[...] += dot(hot, w_out[POS_HI:POS_LO, :]) + dot(hot, w_out[POS_LO:POS_GRAD, :])

        norm(m, rows, xf[...])
        keep_copy("normed", m).start()
        for part in range(3):
            @pl.when(first & (m == 0))
            def _():
                load_in(part).wait()

            cols = slice(part * D, (part + 1) * D)
            proj = dot(a1[0, rows, :], w_in[:, cols])
            if part != 1:
                proj = proj + bi[:, cols].astype(F32)
            slot, at = ((0, D), (2, 0), (2, D))[part]
            a2[slot, rows, at:at + D] = proj.astype(BF)

        @pl.when(first & (m == 0))
        def _():
            load_in(3).wait()

        ends = ends_of(m)
        seg_rows = segment(ends, lax.broadcasted_iota(I32, (ROWS, ROWS), 0))
        seg_cols = segment(ends, lax.broadcasted_iota(I32, (ROWS, ROWS), 1))
        same = seg_rows == seg_cols
        for g in range(D // WIDE):
            lo = D + g * WIDE
            q = spread(a2[0, rows, lo:lo + WIDE])
            k = a2[2, rows, lo - D:lo - D + WIDE]
            v = a2[2, rows, lo:lo + WIDE]
            s = dot_nt(q, k).reshape(GROUP, ROWS, ROWS) * HEAD_DIM ** (-0.5)
            s = jnp.where(same[None], s, MASKED_SCORE)
            s = jnp.exp(s - jnp.max(s, axis=2, keepdims=True))
            p = s * (1.0 / jnp.sum(s, axis=2, keepdims=True))
            p = p.reshape(GROUP * ROWS, ROWS).astype(BF)
            probs_at(m, g)[...] = p
            a2[0, rows, g * WIDE:(g + 1) * WIDE] = gather_heads(dot(p, v)).astype(BF)
        keep_copy("mixed", m).start()
        finish_forward(m, dot(a2[0, rows, 0:D], w_in[:, 3 * D:4 * D]) + bias_out)

    def attention_backward(m):
        rows = rows_of(m)
        backward_copy(m).wait_recv()
        d = ds[0, m]
        slot, cols = half_at(3)
        gs[slot, rows, cols] = d
        vec[0:1, :] += col_sum(d.astype(F32))
        d_mixed = dot(d, w_in_t[3 * D:4 * D, :]).astype(BF)
        for g in range(D // WIDE):
            lo = D + g * WIDE
            q = spread(a2[0, rows, lo:lo + WIDE])
            k = a2[2, rows, lo - D:lo - D + WIDE]
            v = a2[2, rows, lo:lo + WIDE]
            dm = spread(d_mixed[:, g * WIDE:(g + 1) * WIDE])
            p = probs_at(m, g)[...]
            dp_ = dot_nt(dm, v)
            pf = p.astype(F32)
            row_dot = jnp.sum(pf * dp_, axis=1, keepdims=True)
            d_s = (pf * (dp_ - row_dot)).astype(BF)
            dq = (gather_heads(dot(d_s, k)) * HEAD_DIM ** (-0.5)).astype(BF)
            dk = (dot_tn(d_s, q) * HEAD_DIM ** (-0.5)).astype(BF)
            dv = dot_tn(p, dm).astype(BF)
            low = slice(g * WIDE, (g + 1) * WIDE)
            high = slice(D + g * WIDE, D + (g + 1) * WIDE)
            gs[half_at(0)[0], rows, low] = dq
            gs[half_at(1)[0], rows, high] = dk
            gs[half_at(2)[0], rows, low] = dv
            vec_in[0:1, low] += col_sum(dq.astype(F32))
            vs = slice(2 * D + g * WIDE, 2 * D + (g + 1) * WIDE)
            vec_in[0:1, vs] += col_sum(dv.astype(F32))
        keep_copy("inner", m).start()
        d_normed = dot(gs[half_at(0)[0], rows, :], w_in_t[0:2 * D, :])
        d_normed = d_normed + dot(gs[half_at(2)[0], rows, 0:D], w_in_t[2 * D:3 * D, :])
        finish_backward(m, norm_back(m, rows, d_normed, d.astype(F32)))

        @pl.when(first)
        def _():
            at = pl.ds(pl.multiple_of(POS_GRAD + m * KINDS, KINDS), KINDS)
            w_out[at, :] = dot_tn(places(m), xo[m]).astype(BF)

    def hidden_in(rows, part):
        cols = slice(part * D, (part + 1) * D)
        return dot(a1[0, rows, :], w_in[:, cols]) + bi[:, cols].astype(F32)

    def hidden(rows, part, v):
        cdf = 0.5 + 0.5 * lax.erf(v * INV_SQRT2)
        act = (v * cdf).astype(BF)
        for n in range(8):
            chip, core = part * 4 + n // 2, n % 2
            a2[core_slot(core), rows, chip * 128:(chip + 1) * 128] = act[:, n * 128:(n + 1) * 128]
        return act, cdf + v * (INV_SQRT_2PI * jnp.exp(-0.5 * v * v))

    def enter(m, rows):
        forward_copy(m).wait_recv()
        xf[...] = xs[m].astype(F32)
        norm(m, rows, xf[...])
        keep_copy("normed", m).start()

    def second_part(part, act):
        total = None
        for core in (0, 1):
            units = jnp.concatenate(
                [act[:, (2 * n + core) * 128:(2 * n + core + 1) * 128] for n in range(4)], axis=1)
            term = dot(units, w_out[core * HALF + part * 512:core * HALF + (part + 1) * 512, :])
            total = term if total is None else total + term
        return total

    def back_part(part, d_inner):
        return dot(d_inner, w_in_t[part * D:(part + 1) * D, :])

    def leave(m, d, d_normed):
        keep_copy("inner", m).start()
        finish_backward(m, norm_back(m, rows_of(m), d_normed, d.astype(F32)))

    def set_inner(rows, part, d_inner):
        slot, at = half_at(part)
        gs[slot, rows, at] = d_inner
        vec_in[0:1, part * D:(part + 1) * D] += col_sum(d_inner.astype(F32))

    def feed_forward(m):
        rows = rows_of(m)
        enter(m, rows)
        branch, before = bias_out, None
        for part in range(4):
            v = hidden_in(rows, part)
            if before is not None:
                branch = branch + second_part(part - 1, before)
            before, slope = hidden(rows, part, v)
            slot, at = half_at(part)
            gs[slot, rows, at] = slope.astype(BF)
        keep_copy("act", m).start()
        finish_forward(m, branch + second_part(3, before))

    def feed_backward(m):
        rows = rows_of(m)
        backward_copy(m).wait_recv()
        keep_copy("branch", m).start()
        d = ds[0, m]
        vec[0:1, :] += col_sum(d.astype(F32))
        d_normed, before = 0.0, None
        for part in range(4):
            slot, at = half_at(part)
            d_act = dot(d, w_out_t[:, part * D:(part + 1) * D])
            if before is not None:
                d_normed = d_normed + back_part(part - 1, before)
            before = (d_act * gs[slot, rows, at].astype(F32)).astype(BF)
            set_inner(rows, part, before)
        leave(m, d, d_normed + back_part(3, before))

    def last_before(m):
        rows = rows_of(m)
        d = (ds[0, m].astype(F32) * keep_of(m)).astype(BF)
        ds[0, m] = d
        keep_copy("branch", m).start()
        vec[0:1, :] += col_sum(d.astype(F32))

        def step(part, carry):
            slot = jnp.where(part // 2 == c, 0, 2)
            at = pl.ds(pl.multiple_of((part % 2) * D, D), D)
            cols = pl.ds(pl.multiple_of(part * D, D), D)
            gs[slot, rows, at] = dot(d, w_out_t[:, cols]).astype(BF)
            return carry

        lax.fori_loop(0, 4, step, 0)

    def last_both(m):
        rows = rows_of(m)
        enter(m, rows)
        w_out_t[rows, 0:D] = xf[...].astype(BF)
        d_normed, before = 0.0, None
        for part in range(4):
            v = hidden_in(rows, part)
            if before is not None:
                d_normed = d_normed + back_part(part - 1, before)
            slope = hidden(rows, part, v)[1]
            slot, at = half_at(part)
            before = (gs[slot, rows, at].astype(F32) * slope).astype(BF)
            set_inner(rows, part, before)
        leave(m, ds[0, m], d_normed + back_part(3, before))
        keep_copy("act", m).start()

    def last_after(m):
        rows = rows_of(m)
        keep = keep_of(m)

        def step(n, carry):
            cols = pl.ds(pl.multiple_of(n * 512, 512), 512)
            branch = dot(a2[core_slot(0), rows, :], w_out[0:HALF, cols]) + bo[:, cols].astype(F32)
            branch = branch + dot(a2[core_slot(1), rows, :], w_out[HALF:FF, cols])
            out = w_out_t[rows, cols].astype(F32) + branch
            xs[m, :, cols] = out.astype(BF)
            vec[3:4, cols] += col_sum(keep * out * out)
            vec[4:5, cols] += col_sum(keep * branch * branch)
            return carry

        lax.fori_loop(0, 2, step, 0)

    def say_ready():
        for peer in [z_peers[1], z_peers[3], y_peers[1], y_peers[3]] + across:
            pl.semaphore_signal(ready, inc=1, device_id=peer, device_id_type=MESH)


    coords = ((z, y), (y, z), (z, y))
    peers = ((z_peers, y_peers), (y_peers, z_peers), (z_peers, y_peers))
    sets = (0, 1, 2)

    def start_small(height):
        def cross():
            return remote(small.at[:, :, other, 0:height], small_x.at[:, :, 0:height], o_send.at[2],
                          o_recv.at[2], sibling)

        count = jnp.int32(0)
        for k in (1, 2, 3):
            stat_copy(k).wait_recv()
        for j in range(32):
            quad = slice((j // 4) * 128, (j // 4 + 1) * 128)
            at = (j // 8, (j // 2) % 4, j % 2)
            small[at + (slice(0, 1),)] = vec_in[0:1, j * 128:(j + 1) * 128]
            small[at + (slice(1, 4),)] = vec[0:3, quad]
            for s in range(4):
                small[at + (slice(4 + s, 5 + s),)] = stat_s[s, 0:1, :]
        cross().start()
        return cross

    def reduce(block_of, land1_of, land2_of, half, height, make, between, swapped, got):
        def block(s, a, b):
            return small_sum.at[a, b, 0:height] if s == 2 else block_of(s, a, b)

        def land1(s, i, q):
            return small_1.at[i, q, 0:height] if s == 2 else land1_of(s, i, q)

        def land2(s, i):
            return small_2.at[i, 0:height // 2] if s == 2 else land2_of(s, i)

        def target(p, i):
            return {0: (plus(p, 2), 0), 1: (plus(p, 2), 1), 2: (plus(p, 1), 1),
                    3: (plus(p, 3), 0), 4: (plus(p, 1), 0), 5: (plus(p, 3), 1)}[i]

        def step1(s, i, q):
            a, h = target(coords[s][0], i)
            peer = peers[s][0][1 if i % 2 == 0 else 3]
            return remote(block(s, a, 2 * h + q), land1(s, i, q), s1_send.at[s, i, q],
                          s1_recv.at[s, i, q], peer)

        def half_of(s, b, h):
            return block(s, coords[s][0], b).at[h * half[s]:(h + 1) * half[s], :]

        def step2(s, i):
            b, h = target(coords[s][1], i)
            k = 1 if i % 2 == 0 else 3
            if s in swapped and i > 1:
                near = (y_near, z_near)[s]
                slot = (2 if i % 2 == 0 else 4) + c
                return remote(half_of(s, b, h), land2(s, slot), s2_send.at[s, i],
                              s2_recv.at[s, slot], near(k, h))
            return remote(half_of(s, b, h), land2(s, i), s2_send.at[s, i], s2_recv.at[s, i],
                          peers[s][1][k])

        def wait2(s, slot):
            remote(half_of(s, 0, 0), land2(s, slot), s2_send.at[s, slot], s2_recv.at[s, slot],
                   sibling).wait_recv()

        def own_half(s, core):
            return block(s, *coords[s]).at[pl.ds(pl.multiple_of(core * half[s], half[s]), half[s]), :]

        def swap(s):
            return own_copy(s, own_half(s, other), got(s))

        def turn_of(s, h, n):
            high, low = coords[s][1] // 2, coords[s][1] % 2
            early = jnp.where(h == high, 1 - low, low)
            return early if n == 0 else 1 - early

        def wait1(s, i, q):
            remote(block(s, 0, 0), land1(s, i, q), s1_send.at[s, i, q], s1_recv.at[s, i, q],
                   sibling).wait_recv()

        def add(ref, *others):
            total = ref[...].astype(F32)
            for o in others:
                total = total + o[...].astype(F32)
            ref[...] = total.astype(ref.dtype)

        cross = start_small(height)
        def start(s, pieces):
            for k in (0, 1):
                for i in pieces:
                    step1(s, i, turn_of(s, target(0, i)[1], k)).start()

        def chunk(t, carry):
            n = jnp.where(t == 0, 2, jnp.where(t == 1, 1, jnp.where(t == 2, 3, 0)))
            for s in (0, 1):
                make(s, plus(coords[s][0], n))
                if s == 0:
                    @pl.when(t == 0)
                    def _():
                        pl.semaphore_wait(ready, 8)
                        cross().wait_recv()
                        small_sum[:, :, 0:height] = (
                            small[:, :, c, 0:height] + small_x[:, :, 0:height])
                        start(2, (0, 1, 2, 3))
                for when, pieces in ((0, (0, 1)), (1, (2,)), (2, (3,))):
                    @pl.when(t == when)
                    def _():
                        start(s, pieces)
            return carry

        lax.fori_loop(0, 4, chunk, 0)
        for k in (0, 1):
            for i in (4, 5):
                for s in (2, 0, 1):
                    a, h = target(coords[s][0], i)
                    q = turn_of(s, h, k)
                    step1(s, i - 4, q).wait_recv()
                    add(block(s, a, 2 * h + q), land1(s, i - 4, q))
                    step1(s, i, q).start()
        between()
        for n, pieces in ((2, (0, 1)), (1, (2,)), (3, (3,)), (0, ())):
            for s in sets:
                p1, p2 = coords[s]
                b = plus(p2, n)
                h, q = b // 2, b % 2
                up, down = jnp.where(h == 0, 4, 2), jnp.where(h == 0, 3, 5)
                wait1(s, up, q)
                wait1(s, down, q)
                add(block(s, p1, b), land1(s, up, q), land1(s, down, q))
                for i in pieces:
                    step2(s, i).start()
                if n == 0 and s in swapped:
                    swap(s).start()
        for i in (4, 5):
            for s in sets:
                b, h = target(coords[s][1], i)
                step2(s, i - 4).wait_recv()
                add(half_of(s, b, h), land2(s, i - 4))
                step2(s, i).start()
        for s in sets:
            p2 = coords[s][1]
            if s in swapped:
                for slot in (2, 3, 4, 5):
                    wait2(s, slot)
                add(own_half(s, c), land2(s, 2 + c), land2(s, 4 + c))
                swap(s).wait_recv()
                add(got(s), land2(s, 2 + other), land2(s, 4 + other))
                continue
            for h, up, down in ((0, 4, 3), (1, 2, 5)):
                step2(s, up).wait_recv()
                step2(s, down).wait_recv()
                add(half_of(s, p2, h), land2(s, up), land2(s, down))
        small_o[...] = small_sum[z, y, 0:8]

        def finish():
            cross().wait_send()
            for s in sets:
                for i in range(6):
                    for q in (0, 1):
                        step1(s, i, q).wait_send()
                    step2(s, i).wait_send()
                if s in swapped:
                    swap(s).wait_send()

        return finish

    def stat_copy(k):
        return remote(stat_s.at[sec], stat_s.at[sec], x_send.at[k - 1], x_recv.at[k - 1],
                      x_peers[k])

    def send_stats():
        count = jnp.int32(0)
        for m in range(MICRO):
            count = count + ends_of(m)[2]
        lanes = lax.broadcasted_iota(I32, (8, 128), 1)
        stream_sq = jnp.sum(vec[3:4, :], axis=1, keepdims=True)
        branch_sq = jnp.sum(vec[4:5, :], axis=1, keepdims=True)
        stat_s[sec] = jnp.where(
            lanes == 0, stream_sq,
            jnp.where(lanes == 1, branch_sq, jnp.where(lanes == 2, count.astype(F32), 0.0)))
        for k in (1, 2, 3):
            stat_copy(k).start()

    def both(ref, start, width, *cols):
        return ref[:, :, pl.ds(pl.multiple_of(start, width), width)].reshape(2 * ALL, width).T

    def kept(n):
        for m in range(MICRO):
            keep_copy(n, m).wait_recv()

    def kept_sent(n):
        for m in range(MICRO):
            keep_copy(n, m).wait_send()

    def pos_copy(k):
        return remote(pos_s, pos_s, x_send.at[2 + k], x_recv.at[3], x_peers[k])

    def own_copy(n, src, dst):
        return remote(src, dst, o_send.at[n], o_recv.at[n], sibling)

    @pl.when(first)
    def _():
        build_blend()
        high, low = split(blend[0:SHORT, :])
        rows = dot_tn(high, table[...]) + dot_tn(low, table[...])
        w_out[POS_HI:POS_LO, :], w_out[POS_LO:POS_GRAD, :] = split(rows)
        load_x.wait()

    pl.semaphore_wait(barrier, len(partners))

    @pl.when(is_att)
    def _():
        @pl.when(sec > 0)
        def _():
            for part in range(4):
                load_in(part).wait()
            transpose_in()

        def turn_second():
            kept("normed")
            kept("mixed")

            def step(zz, carry):
                at = pl.ds(pl.multiple_of(zz * 256, 256), 256)
                w_out_t[at, 2 * D:2 * D + 2 * ALL] = jnp.where(
                    c == 0, both(a1, zz * 256, 256), both(a2.at[0:2], zz * 256, 256))
                return carry

            lax.fori_loop(0, 4, step, 0)

        def tick(t, carry):
            early = (sec == 2) & (t == MICRO - 1)
            late = (sec == 2) & (t == MICRO)
            is_fwd = ((t < MICRO) & jnp.logical_not(early)) | late
            m = jnp.where(early, 0, jnp.where(late, MICRO - 1, t % MICRO))

            @pl.when(is_fwd)
            def _():
                attention_forward(m)

            @pl.when(is_fwd & (m == MICRO - 1))
            def _():
                @pl.when(first)
                def _():
                    transpose_in()

                send_stats()
                say_ready()

                @pl.when(first)
                def _():
                    turn_second()

            @pl.when(jnp.logical_not(is_fwd))
            def _():
                attention_backward(m)

            return carry

        lax.fori_loop(0, 2 * MICRO, tick, 0)

        @pl.when(first)
        def _():
            own_edge(0, input_s).start()

        @pl.when(sec > 0)
        def _():
            turn_second()

        kept("inner")

        def block(s, a, b):
            zz, yy = (a, b) if s == 0 else (b, a)
            at = pl.ds(pl.multiple_of(zz * 256 + yy * 64, 64), 64)
            return w_out_t.at[at, s * D:(s + 1) * D]

        def land1(s, i, q):
            at = pl.ds(pl.multiple_of((i * 2 + q) * 64, 64), 64)
            return w_in.at[at, s * HALF:s * HALF + D]

        def land2(s, i):
            at = pl.ds(pl.multiple_of(768 + i * 32, 32), 32)
            return w_in.at[at, s * HALF:s * HALF + D]

        def make(s, a):
            if s == 1:
                lhs = jnp.concatenate([
                    w_out_t[pl.ds(pl.multiple_of(zz * 256 + a * 64, 64), 64), 2 * D:2 * D + 2 * ALL]
                    for zz in range(4)], axis=0)
                rhs = gs[0:2, :, D:2 * D].reshape(2 * ALL, D)
                made = dot(lhs, rhs).astype(BF)
                for zz in range(4):
                    w_out_t[pl.ds(pl.multiple_of(zz * 256 + a * 64, 64), 64), D:2 * D] = (
                        made[zz * 64:(zz + 1) * 64, :])
            else:
                at = pl.ds(pl.multiple_of(a * 256, 256), 256)
                lhs = both(a1, a * 256, 256)
                rhs = gs[0:2, :, 0:D].reshape(2 * ALL, D)
                w_out_t[at, 0:D] = dot(lhs, rhs).astype(BF)

        small[...] = jnp.zeros_like(small)

        @pl.when(first)
        def _():
            total = jnp.zeros((128, D), F32)
            grads = w_out[POS_GRAD:POS_GRAD + MICRO * KINDS, :].reshape(MICRO, KINDS, D)
            b_hi, b_lo = split(blend[...])
            for m in range(MICRO):
                total = total + dot(b_hi, grads[m]) + dot(b_lo, grads[m])
            for pair in (0, 1):
                both_sections = jnp.concatenate(
                    [total[0:64, (2 * pair + n) * 256:(2 * pair + n + 1) * 256] for n in (0, 1)],
                    axis=0)
                at = slice(8 + pair * 8, 16 + pair * 8)
                small[:, :, :, at] = both_sections.T.reshape(4, 4, 2, 8, 128)

        def got(n):
            return got_in.at[:, n * D:(n + 1) * D]

        finish = reduce(block, land1, land2, (32, 32, 16), 32, make, lambda: None, (0, 1), got)

        @pl.when(first)
        def _():
            pos_s[...] = small_sum[z, y, 8:24]
            for k in (1, 2, 3):
                pos_copy(k).start()

        def mine(n):
            return block(n, *coords[n]).at[pl.ds(pl.multiple_of(c * 32, 32), 32), :]

        copies = [
            pltpu.make_async_copy(mine(n), gin_o.at[c, :, n * D:(n + 1) * D], out_sem.at[n])
            for n in (0, 1)]
        copies.append(pltpu.make_async_copy(got_in, gin_o.at[other], out_sem.at[2]))
        for copy in copies:
            copy.start()
        finish()
        for copy in copies:
            copy.wait()
        kept_sent("normed")
        kept_sent("mixed")
        kept_sent("inner")

    @pl.when(is_ff)
    def _():
        for part in range(4):
            load_in(part).wait()

        def arrived(n, carry):
            load_out(n).wait()
            return carry

        lax.fori_loop(0, 32, arrived, 0)

        def each(work):
            def step(m, carry):
                work(m)
                return carry

            lax.fori_loop(0, MICRO, step, 0)

        @pl.when(last)
        def _():
            load_d.wait()
            transpose_out()
            transpose_in()
            each(last_before)
            each(last_both)
            each(last_after)

        @pl.when(jnp.logical_not(last))
        def _():
            each(feed_forward)
            transpose_out()
            transpose_in()

        say_ready()
        send_stats()

        @pl.when(jnp.logical_not(last))
        def _():
            each(feed_backward)

        for n in ("normed", "act", "branch", "inner"):
            kept(n)

        def block(s, a, b):
            if s == 0:
                at = pl.ds(pl.multiple_of(a * 256 + b * 64, 64), 64)
                return w_out_t.at[at, 0:HALF]
            at = pl.ds(pl.multiple_of(b * 512 + a * 128, 128), 128)
            return w_in_t.at[at, :]

        def land1(s, i, q):
            n = i * 2 + q
            if s == 0:
                return w_in.at[pl.ds(pl.multiple_of(n * 64, 64), 64), 0:HALF]
            rows = pl.ds(pl.multiple_of((n % 8) * 128, 128), 128)
            return w_in.at[rows, pl.ds(pl.multiple_of(HALF + (n // 8) * D, D), D)]

        def land2(s, i):
            if s == 0:
                return w_in.at[pl.ds(pl.multiple_of(768 + i * 32, 32), 32), 0:HALF]
            return w_in.at[512 + i * 64:512 + (i + 1) * 64, FF - D:FF]

        def make(s, a):
            if s == 0:
                at = pl.ds(pl.multiple_of(a * 256, 256), 256)
                lhs = both(a1, a * 256, 256)
                for n in (0, 1):
                    cols = slice(n * D, (n + 1) * D)
                    rhs = gs[0:2, :, cols].reshape(2 * ALL, D)
                    w_out_t[at, cols] = dot(lhs, rhs).astype(BF)
            else:
                def step(pair, carry):
                    lhs = []
                    for n in (0, 1):
                        chip = (pair * 2 + n) * 4 + a
                        lhs.append(both(a2.at[0:2], chip * 128, 128))
                    rhs = ds[...].reshape(2 * ALL, D)
                    block2 = dot(jnp.concatenate(lhs, axis=0), rhs).astype(BF)
                    for n in (0, 1):
                        chip = (pair * 2 + n) * 4 + a
                        at = pl.ds(pl.multiple_of(chip * 128, 128), 128)
                        w_in_t[at, :] = block2[n * 128:(n + 1) * 128, :]
                    return carry

                lax.fori_loop(0, 2, step, 0)

        small[...] = jnp.zeros_like(small)
        def between():
            @pl.when(last)
            def _():
                for k in (1, 2, 3):
                    layer_copy(k).start()
                own_edge(3, layer_s).start()

        finish = reduce(block, land1, land2, (32, 64, 8), 16, make, between, (0,),
                        lambda s: got_in)

        def part(core):
            return block(0, z, y).at[pl.ds(pl.multiple_of(core * 32, 32), 32), :]

        copies = [
            pltpu.make_async_copy(src, dst, out_sem.at[n]) for n, (src, dst) in enumerate((
                (part(c), gin_o.at[c]), (got_in, gin_o.at[other]), (block(1, y, z), gout_o)))]
        for copy in copies:
            copy.start()
        finish()
        for copy in copies:
            copy.wait()
        for n in ("normed", "act", "branch", "inner"):
            kept_sent(n)

    @pl.when(first)
    def _():
        own_edge(0, input_s).wait()
        layer_copy(1).wait_recv()

    @pl.when(sec > 0)
    def _():
        for m in range(MICRO):
            input_copy(1, m).wait_recv()

        @pl.when(sec < 3)
        def _():
            layer_copy(1).wait_recv()

        @pl.when(last)
        def _():
            own_edge(3, layer_s).wait()

    outs = [pltpu.make_async_copy(layer_s, layer_o, out_sem.at[3]),
            pltpu.make_async_copy(input_s, input_o, out_sem.at[4])]
    for copy in outs:
        copy.start()

    @pl.when(sec > 0)
    def _():
        pos_copy(1).wait_recv()

        for m in range(MICRO):
            backward_copy(m).wait_send()

    gpos_o[...] = pos_s[...]
    for k in (1, 2, 3):
        stat_copy(k).wait_send()

    @pl.when(first)
    def _():
        for k in (1, 2, 3):
            pos_copy(k).wait_send()
            for m in range(MICRO):
                input_copy(k, m).wait_send()

    @pl.when(last)
    def _():
        for k in (1, 2, 3):
            layer_copy(k).wait_send()

    for copy in outs:
        copy.wait()


def output_kernel(
    layer, inp, gin, gout, small, gpos,
    layer_o, input_o, gin_o, gout_o, bin_o, bout_o, gain_o, shift_o, pos_o, stats_o,
):
    sec = lax.axis_index("section")
    quarter = lax.axis_index("dp") % 4
    layer_o[...] = layer[...]
    input_o[...] = inp[...]
    for half in (0, 1):
        gin_o[0, :, half * HALF:(half + 1) * HALF] = gin[half].astype(F32)

    @pl.when(sec % 2 == 0)
    def _():
        gout_o[...] = jnp.zeros_like(gout_o)

    @pl.when(sec % 2 == 1)
    def _():
        gout_o[0] = gout[...].astype(F32)

    bin_o[...] = small[0:1, :]
    for row, ref in ((1, bout_o), (2, gain_o), (3, shift_o)):
        line = small[row:row + 1, :]
        picked = line[:, 0:32]
        for n in (1, 2, 3):
            picked = jnp.where(quarter == n, line[:, n * 32:(n + 1) * 32], picked)
        ref[...] = picked
    pair = jnp.where(sec < 2, gpos[0:8, :], gpos[8:16, :])
    pos_o[...] = jnp.where(sec % 2 == 0, pair[:, 0:SHORT], pair[:, 64:64 + SHORT])
    count = small[4:5, 2:3]
    kind = lax.broadcasted_iota(I32, (2, 4), 0)
    section = lax.broadcasted_iota(I32, (2, 4), 1)
    total = jnp.zeros((2, 4), F32)
    for s in range(4):
        for r in range(2):
            total = jnp.where(
                (kind == r) & (section == s), small[4 + s:5 + s, r:r + 1], total)
    stats_o[...] = jnp.sqrt(total / (count * D))


def local(inputs, cotangent, layout, pos_index, pos_table, slab_in, slab_out, bias_in, bias_out,
          ln_gain, ln_bias):
    shape = jax.ShapeDtypeStruct
    vmem = pl.BlockSpec(memory_space=pltpu.VMEM)
    smem = pl.BlockSpec(memory_space=pltpu.SMEM)
    anywhere = pl.BlockSpec(memory_space=pl.ANY)
    dma = pltpu.SemaphoreType.DMA

    parts = pl.pallas_call(
        train_kernel,
        name="train",
        out_shape=(
            shape((MICRO, ROWS, 256), BF), shape((MICRO, ROWS, 256), BF), shape((2, 32, HALF), BF), shape((128, D), BF),
            shape((8, 128), F32), shape((16, 128), F32)),
        in_specs=[smem] + [anywhere] * 4 + [vmem] * 6,
        out_specs=(anywhere,) * 4 + (vmem,) * 2,
        scratch_shapes=[
            pltpu.VMEM((D, FF), BF), pltpu.VMEM((FF, D), BF),
            pltpu.VMEM((FF, D), BF), pltpu.VMEM((D, FF), BF),
            pltpu.VMEM((MICRO, ROWS, D), BF), pltpu.VMEM((2, MICRO, ROWS, D), BF),
            pltpu.VMEM((MICRO, ROWS, D), BF),
            pltpu.VMEM((2, ALL, D), BF), pltpu.VMEM((3, ALL, HALF), BF),
            pltpu.VMEM((3, ALL, HALF), BF),
            pltpu.VMEM((ROWS, 128), F32), pltpu.VMEM((ROWS, D), F32),
            pltpu.VMEM((8, FF), F32), pltpu.VMEM((8, D), F32), pltpu.VMEM((128, KINDS), F32),
            pltpu.VMEM((32, HALF), BF),
            pltpu.VMEM((4, 4, 2, 32, 128), F32), pltpu.VMEM((4, 4, 32, 128), F32),
            pltpu.VMEM((4, 4, 32, 128), F32), pltpu.VMEM((6, 2, 32, 128), F32),
            pltpu.VMEM((6, 16, 128), F32), pltpu.VMEM((4, 8, 128), F32),
            pltpu.VMEM((16, 128), F32),
            pltpu.VMEM((MICRO, ROWS, 256), BF), pltpu.VMEM((MICRO, ROWS, 256), BF),
            dma((6,)), dma((32,)), dma((MICRO,)), dma((MICRO,)), dma((MICRO,)), dma((MICRO,)),
            dma((4, MICRO)), dma((4, MICRO)), pltpu.SemaphoreType.REGULAR,
            dma((3, 6, 2)), dma((3, 6, 2)), dma((3, 6)), dma((3, 6)), dma((3,)), dma((3,)),
            dma((6,)), dma((4,)), dma((3,)), dma((3, MICRO)), dma((MICRO + 1,)), dma((1,)), dma((5,)),
        ],
        compiler_params=pltpu.CompilerParams(
            collective_id=0, has_side_effects=True, vmem_limit_bytes=64 * MIB - 65536),
    )(layout.transpose(2, 1, 0), inputs, cotangent, slab_in, slab_out, bias_in, bias_out, ln_gain,
      ln_bias, pos_index.T, pos_table)

    *grads, grad_pos, stats = pl.pallas_call(
        output_kernel,
        name="outputs",
        out_shape=(
            shape((MICRO, ROWS, 256), BF), shape((MICRO, ROWS, 256), BF), shape((1, 32, FF), F32),
            shape((1, 128, D), F32), shape((1, 128), F32), shape((1, 32), F32),
            shape((1, 32), F32), shape((1, 32), F32), shape((8, SHORT), F32), shape((2, 4), F32)),
        in_specs=[vmem] * 6,
        out_specs=(vmem,) * 10,
        compiler_params=pltpu.CompilerParams(vmem_limit_bytes=60 * MIB),
    )(*parts)
    return (*grads, grad_pos.T, stats)


def solution(mesh):
    return jax.shard_map(
        local,
        mesh=mesh,
        in_specs=(
            P(None, "dp", None), P(None, "dp", None), P(None, "dp", None), P(), P(),
            P("section", None, None), P("section", None, None), P("section", None),
            P("section", None), P("section", None), P("section", None)),
        out_specs=(
            P(None, "dp", "section"), P(None, "dp", "section"), P("section", "dp", None),
            P("section", "dp", None), P("section", "dp"), P("section", "dp"),
            P("section", "dp"), P("section", "dp"), P(None, ("section", "dp")), P()),
        check_vma=False,
    )
```
